32 devices in a mesh: pair: 4 (over y, x), col: 8 (over z, core).
Axes of the slice: x: 2, y: 2, z: 4, core: 2. Of those that a mesh axis runs over, the one named last changes fastest.
Arguments:
- amplitudes: float32 [2048, 2048], P('pair', 'col'), may hold values from -6 to 6
- integrals: float32 [2048, 2048], P('pair', 'col'), may hold values from -0.25 to 0.25
- amp_tiles: int32 [4, 8, 4], P('pair', 'col'), may hold values from 0 to 7, as said below
- amp_count: int32 [4, 8], P('pair', 'col'), may hold values from 1 to 4, as said below
- int_mask: int32 [16, 16], P('pair', 'col'), may hold values 0 or 1
Outputs:
- ladder: float32 [2048, 2048], P('pair', 'col')
The draws below stay inside these ranges and needn't reach their ends.
Inputs may be any that keep to these rules, and one draw needn't show every extreme that they name: `amp_tiles`: in each device's list the entries are distinct tile numbers of that device's block. `amp_count`: some device's count equals 4 in every draw.
All inputs are finite; a program needn't handle non-finite values. No bound on the sum of `int_mask` on one device may be relied on, other than what follows from the above.
Results may differ from the reference program's by a relative error of at most 0.00007.
Values sent between devices are 32-bit elements; how exact they have to be, the bound alone decides.
A program may use at most 128 MiB of HBM per device.

```python
import jax
import jax.numpy as jnp
from jax import lax

TILE = 128
PT_DEV = 4
KT_COL = 2
LIVE = 4
P_SIZE = 2048
K = 2048
N = 2048
KT = 16
NT = 16
N_PAIR = 4
N_COL = 8


def draw_amp_tiles(key, part):
    key_list = jax.random.split(key, N_PAIR * N_COL)

    def draw_one(subkey):
        return jax.random.permutation(subkey, PT_DEV * KT_COL)[:LIVE]
    chosen = jax.vmap(draw_one)(key_list)
    return chosen.astype(jnp.int32).reshape(N_PAIR, N_COL, LIVE)


def draw_amp_count(key, part):
    key_first, key_second = jax.random.split(key)
    counts = jax.random.randint(key_first, (N_PAIR * N_COL,), 1, LIVE + 1)
    full_at = jax.random.randint(key_second, (), 0, N_PAIR * N_COL)
    counts = jnp.where(jnp.arange(N_PAIR * N_COL) == full_at, LIVE, counts)
    return counts.reshape(N_PAIR, N_COL).astype(jnp.int32)


def set_ends(values, own_key, low, high):
    longest = values.shape.index(max(values.shape))
    spots = []
    for shift in (0, 1):
        where = [jax.random.randint(jax.random.fold_in(own_key, axis), (), 0, length) for axis, length in enumerate(values.shape)]
        where[longest] = (where[longest] + shift) % values.shape[longest]
        spots.append(tuple(where))
    return values.at[spots[0]].set(low).at[spots[1]].set(high)


def level_of(stream_key, dims, shards, smallest, largest):
    def one(axis_at, parts):
        draws = jax.random.uniform(jax.random.fold_in(jax.random.fold_in(stream_key, 6), axis_at), (parts,), jnp.float32, smallest / len(shards), largest / len(shards))
        return jnp.repeat(jnp.exp(draws), dims[axis_at] // parts).reshape((-1,) + (1,) * (len(dims) - axis_at - 1))

    level = one(*shards[0])
    for cut in shards[1:]:
        level = level * one(*cut)
    return level


def bell_draw(stream_key, extent, scale, bound, cuts=(), kind=jnp.bfloat16):
    drawn = scale * jax.random.normal(stream_key, extent, jnp.float32)
    if cuts:
        drawn = drawn * level_of(stream_key, extent, cuts, -0.22, 0.18)
    return jnp.clip(drawn, -bound, bound).astype(kind)


def setup_inputs(seed: int = 0) -> dict:
    keys = jax.random.split(jax.random.key(seed), 6)
    return {
        "amplitudes": bell_draw(keys[0], (P_SIZE, K), 1.0, 6.0, ((0, 4), (1, 8)), jnp.float32),
        "integrals": bell_draw(keys[1], (K, N), (K // 4) ** -0.5, 0.25, ((0, 4), (1, 8)), jnp.float32),
        "amp_tiles": draw_amp_tiles(jax.random.fold_in(keys[5], 71), 0),
        "amp_count": draw_amp_count(jax.random.fold_in(keys[5], 71), 0),
        "int_mask": set_ends((jax.random.randint(keys[4], (KT, NT), 0, 2) < 1).astype(jnp.int32), jax.random.fold_in(keys[4], 1), 0, 1),
    }


def expand_tiles(tile_mask):
    row_tiles = tile_mask.shape[0]
    col_tiles = tile_mask.shape[1]
    widened = jnp.broadcast_to(tile_mask[:, None, :, None], (row_tiles, TILE, col_tiles, TILE))
    return widened.reshape(row_tiles * TILE, col_tiles * TILE)


def occupancy(amp_tiles, amp_count):
    slot_index = jnp.arange(LIVE, dtype=jnp.int32)
    is_live = slot_index[None, None, :] < amp_count[:, :, None]
    tile_ids = jnp.arange(PT_DEV * KT_COL, dtype=jnp.int32)
    matches = (amp_tiles[:, :, :, None] == tile_ids[None, None, None, :]) & is_live[:, :, :, None]
    occupied = jnp.max(matches.astype(jnp.float32), axis=2)
    occupied = occupied.reshape(N_PAIR, N_COL, PT_DEV, KT_COL).transpose(0, 2, 1, 3)
    return occupied.reshape(N_PAIR * PT_DEV, N_COL * KT_COL)


def reference(amplitudes, integrals, amp_tiles, amp_count, int_mask):
    amp_sparse = amplitudes * expand_tiles(occupancy(amp_tiles, amp_count))
    int_sparse = integrals * expand_tiles(int_mask.astype(jnp.float32))
    return jnp.dot(amp_sparse, int_sparse, precision=lax.Precision.HIGHEST, preferred_element_type=jnp.float32)
```

```python
import functools

import jax
import jax.numpy as jnp
from jax import lax
from jax.experimental import pallas as pl
from jax.experimental.pallas import tpu as pltpu
from jax.sharding import PartitionSpec as P

TILE = 128
CORES = 2
MESH = pl.DeviceIdType.MESH
BF16 = jnp.bfloat16
F32 = jnp.float32


def split(value):
    high = value.astype(BF16)
    return high, (value - high.astype(F32)).astype(BF16)


def when(*conditions):
    together = conditions[0]
    for condition in conditions[1:]:
        together = jnp.logical_and(together, condition)
    return pl.when(together)


def kernel(
    n_pair, n_col, list_ref, count_ref, mask_ref, amp_hbm, int_hbm, out_ref,
    amp, packed, slots, ints, a_high, a_low, b_high, b_low,
    load_amp, load_int, amp_recv, amp_send, slot_recv, slot_send, int_recv, int_send,
):
    live = packed.shape[1]
    rows, depth = amp.shape
    tile_cols = depth // TILE
    tiles = (rows // TILE) * tile_cols
    int_rows, int_cols = ints.shape[1:]
    half = int_rows // 2
    piece = TILE
    pieces = half // piece

    pair, col = lax.axis_index("pair"), lax.axis_index("col")
    line, line_at, core = n_col // CORES, col // CORES, col % CORES
    wide = n_pair // 2
    high_at, low_at = pair // wide, pair % wide

    sibling = {"col": line_at * CORES + 1 - core}
    above, below = {"col": col + CORES}, {"col": col - CORES}
    across = {"pair": (1 - high_at) * wide + low_at}
    right, left = {"pair": pair + 1}, {"pair": pair - 1}
    has_above, has_below = line_at < line - 1, line_at > 0
    has_right, has_left = low_at < wide - 1, low_at > 0

    int_loads = [
        pltpu.make_async_copy(
            int_hbm.at[pl.ds(at * piece, piece)],
            ints.at[pair, pl.ds(at * piece, piece)],
            load_int.at[at],
        )
        for at in range(2 * pieces)
    ]
    amp_load = pltpu.make_async_copy(amp_hbm, amp, load_amp)
    amp_load.start()
    for load in int_loads:
        load.start()

    barrier = pltpu.get_barrier_semaphore()
    partners = (
        (sibling, None), (across, None), (above, has_above), (below, has_below),
        (right, has_right), (left, has_left),
    )
    for partner, exists in partners:
        def greet(partner=partner):
            pl.semaphore_signal(barrier, inc=1, device_id=partner, device_id_type=MESH)
        if exists is None:
            greet()
        else:
            pl.when(exists)(greet)
    peers = 2
    for _, exists in partners[2:]:
        peers += jnp.where(exists, 1, 0)
    pl.semaphore_wait(barrier, peers)

    def amp_copy(source, slot, way, target):
        ref = packed.at[source, slot]
        return pltpu.make_async_remote_copy(
            src_ref=ref, dst_ref=ref,
            send_sem=amp_send.at[way, source, slot], recv_sem=amp_recv.at[source, slot],
            device_id=target, device_id_type=MESH,
        )

    def slot_copy(source, way, target):
        ref = slots.at[source]
        return pltpu.make_async_remote_copy(
            src_ref=ref, dst_ref=ref,
            send_sem=slot_send.at[way, source], recv_sem=slot_recv.at[source],
            device_id=target, device_id_type=MESH,
        )

    def int_copy(source, at, way, target):
        ref = ints.at[source, pl.ds(at * piece, piece)]
        return pltpu.make_async_remote_copy(
            src_ref=ref, dst_ref=ref,
            send_sem=int_send.at[way, source, at], recv_sem=int_recv.at[source, at],
            device_id=target, device_id_type=MESH,
        )

    amp_load.wait()
    numbers = [
        jnp.where(
            jnp.full((1, TILE), count_ref[0], jnp.int32) > s,
            jnp.full((1, TILE), list_ref[s], jnp.int32),
            -1,
        )
        for s in range(live)
    ]
    for t in range(tiles):
        place = jnp.full((1, TILE), -1, jnp.int32)
        for s in range(live):
            place = jnp.where(numbers[s] == t, s, place)
        slots[col, pl.ds(t, 1), :] = place

    def send_own_amp(copy):
        pl.when(has_above)(lambda: copy(0, above).start())
        pl.when(has_below)(lambda: copy(1, below).start())
        copy(2, sibling).start()

    send_own_amp(lambda way, target: slot_copy(col, way, target))
    for s in range(live):
        number = jnp.broadcast_to(numbers[s], (TILE, TILE))
        value = jnp.zeros((TILE, TILE), F32)
        for t in range(tiles):
            at = (pl.ds(t // tile_cols * TILE, TILE), pl.ds(t % tile_cols * TILE, TILE))
            value = jnp.where(number == t, amp[at], value)
        packed[col, s] = value
        send_own_amp(lambda way, target, s=s: amp_copy(col, s, way, target))

    def ready(at):
        int_loads[at].wait()
        span = pl.ds(at * piece, piece)
        for c in range(int_cols // TILE):
            keep = mask_ref[at * piece // TILE, c].astype(F32)
            cols = pl.ds(c * TILE, TILE)
            ints[pair, span, cols] = ints[pair, span, cols] * keep

    def send_row(source, at):
        pl.when(has_right)(lambda: int_copy(source, at, 0, right).start())
        pl.when(has_left)(lambda: int_copy(source, at, 1, left).start())

    for u in range(pieces):
        ready(u)
        send_row(pair, u)
        ready(pieces + u)
        int_copy(pair, pieces + u, 2, across).start()
    for u in range(pieces):
        send_row(pair, pieces + u)
        int_copy(pair, u, 2, across).start()

    out_ref[...] = jnp.zeros_like(out_ref)

    def amp_slot(source):
        return jnp.abs(source // CORES - line_at)

    def int_slot(source, part):
        away = jnp.abs(source % wide - low_at)
        same = source // wide == high_at
        near = jnp.where(part == 0, away, jnp.where(away > 0, away + 1, 0))
        far = jnp.where(part == 0, away + 2, jnp.where(away > 0, away + 2, 1))
        return jnp.where(same, near, far)

    def step(now, _):
        def pass_amp(source, exists, way, target, more):
            @when(now >= 1, exists)
            def _():
                slot_copy(source, way, target).wait_recv()
                pl.when(more)(lambda: slot_copy(source, way, target).start())
                slot_copy(source, 2, sibling).start()

        def pass_tile(source, s, exists, way, target, more):
            @when(now >= 1, exists)
            def _():
                amp_copy(source, s, way, target).wait_recv()
                pl.when(more)(lambda: amp_copy(source, s, way, target).start())
                amp_copy(source, s, 2, sibling).start()

        def pass_row(source, at, away, across_too):
            def one(side, exists, way, target, more):
                origin = source + side * away

                @when(away >= 1, exists)
                def _():
                    int_copy(origin, at, way, target).wait_recv()
                    pl.when(more)(lambda: int_copy(origin, at, way, target).start())
                    if across_too:
                        int_copy(origin, at, 2, across).start()

            one(-1, low_at - away >= 0, 0, right, has_right)
            one(1, low_at + away < wide, 1, left, has_left)

        lower, upper = col - CORES * now, col + CORES * now
        pass_amp(lower, line_at - now >= 0, 0, above, has_above)
        pass_amp(upper, line_at + now < line, 1, below, has_below)
        other = (1 - high_at) * wide + low_at
        for s in range(max(live, pieces)):
            if s < live:
                pass_tile(lower, s, line_at - now >= 0, 0, above, has_above)
                pass_tile(upper, s, line_at + now < line, 1, below, has_below)
            if s < pieces:
                pass_row(pair, s, now, True)

                @when(now == 1)
                def _(s=s):
                    int_copy(other, pieces + s, 2, across).wait_recv()
                    send_row(other, pieces + s)

        for u in range(pieces):
            pass_row(pair, pieces + u, now - 1, False)
            pass_row(other, pieces + u, now - 2, False)
            away = now - 2
            pl.when(away == 0)(lambda u=u: int_copy(other, u, 2, across).wait_recv())
            for side, exists in ((-1, low_at - away >= 0), (1, low_at + away < wide)):
                @when(away >= 1, exists)
                def _(side=side, u=u, away=away):
                    int_copy(other + side * away, u, 2, across).wait_recv()

        def from_sibling(source):
            slot_copy(source, 2, sibling).wait_recv()
            for s in range(live):
                amp_copy(source, s, 2, sibling).wait_recv()

        mate = line_at * CORES + 1 - core
        pl.when(line_at - now >= 0)(lambda: from_sibling(mate - CORES * now))
        when(now >= 1, line_at + now < line)(lambda: from_sibling(mate + CORES * now))

        @pl.loop(0, n_col)
        def _(source):
            @pl.when(amp_slot(source) == now)
            def _():
                for t in range(tiles):
                    place = jnp.broadcast_to(slots[source, pl.ds(t, 1), :], (TILE, TILE))
                    value = jnp.zeros((TILE, TILE), F32)
                    for s in range(live):
                        value = jnp.where(place == s, packed[source, s], value)
                    at = (pl.ds(t // tile_cols * TILE, TILE), pl.ds(t % tile_cols * TILE, TILE))
                    a_high[(source, *at)], a_low[(source, *at)] = split(value)

        @pl.loop(0, n_pair * 2)
        def _(block):
            source, part = block // 2, block % 2

            @pl.when(int_slot(source, part) == now)
            def _():
                span = pl.ds(pl.multiple_of(part * half, half), half)
                value = ints[source, span]
                b_high[source, span], b_low[source, span] = split(value)

        @pl.loop(0, n_col)
        def _(source):
            start = source * depth
            origin, offset = start // int_rows, start % int_rows
            due = jnp.maximum(amp_slot(source), int_slot(origin, offset // half))

            @pl.when(due == now)
            def _():
                span = pl.ds(pl.multiple_of(offset, depth), depth)
                high, low = b_high[origin, span], b_low[origin, span]
                first = a_high[source]
                total = jnp.dot(first, high, preferred_element_type=F32)
                total += jnp.dot(first, low, preferred_element_type=F32)
                total += jnp.dot(a_low[source], high, preferred_element_type=F32)
                out_ref[...] += total

        return 0

    steps = max(line - 1, wide + 1)
    lax.fori_loop(0, steps + 1, step, 0)

    @pl.loop(0, n_col)
    def _(source):
        mine = source % CORES == core
        at = source // CORES

        def drain(way, target):
            slot_copy(source, way, target).wait_send()
            for s in range(live):
                amp_copy(source, s, way, target).wait_send()

        when(mine, at <= line_at, has_above)(lambda: drain(0, above))
        when(mine, at >= line_at, has_below)(lambda: drain(1, below))
        pl.when(mine)(lambda: drain(2, sibling))

    @pl.loop(0, n_pair)
    def _(source):
        same = source // wide == high_at
        at = source % wide

        def drain(first, way, target):
            for u in range(pieces):
                int_copy(source, first + u, way, target).wait_send()

        when(same, at <= low_at, has_right)(lambda: drain(0, 0, right))
        when(same, at >= low_at, has_left)(lambda: drain(0, 1, left))
        pl.when(same)(lambda: drain(0, 2, across))
        when(at <= low_at, has_right)(lambda: drain(pieces, 0, right))
        when(at >= low_at, has_left)(lambda: drain(pieces, 1, left))
        pl.when(source == pair)(lambda: drain(pieces, 2, across))


def local(n_pair, n_col, amplitudes, integrals, amp_tiles, amp_count, int_mask):
    rows, depth = amplitudes.shape
    int_rows, int_cols = integrals.shape
    live = amp_tiles.shape[-1]
    tiles = (rows // TILE) * (depth // TILE)
    half = int_rows // 2
    assert n_pair % 2 == 0 and n_col % CORES == 0
    assert half % depth == 0 and half % TILE == 0
    pieces = int_rows // TILE
    scratch = [
        pltpu.VMEM((rows, depth), F32),
        pltpu.VMEM((n_col, live, TILE, TILE), F32),
        pltpu.VMEM((n_col, tiles, TILE), jnp.int32),
        pltpu.VMEM((n_pair, int_rows, int_cols), F32),
        pltpu.VMEM((n_col, rows, depth), BF16),
        pltpu.VMEM((n_col, rows, depth), BF16),
        pltpu.VMEM((n_pair, int_rows, int_cols), BF16),
        pltpu.VMEM((n_pair, int_rows, int_cols), BF16),
        pltpu.SemaphoreType.DMA,
        pltpu.SemaphoreType.DMA((pieces,)),
        pltpu.SemaphoreType.DMA((n_col, live)),
        pltpu.SemaphoreType.DMA((3, n_col, live)),
        pltpu.SemaphoreType.DMA((n_col,)),
        pltpu.SemaphoreType.DMA((3, n_col)),
        pltpu.SemaphoreType.DMA((n_pair, pieces)),
        pltpu.SemaphoreType.DMA((3, n_pair, pieces)),
    ]
    held = n_col * (live * TILE * TILE * 4 + rows * depth * 4 + 8 * tiles * TILE)
    held += n_pair * int_rows * int_cols * 8 + 3 * rows * (depth + int_cols) * 4
    any_space = pl.BlockSpec(memory_space=pl.ANY)
    scalar = pl.BlockSpec(memory_space=pltpu.SMEM)
    return pl.pallas_call(
        functools.partial(kernel, n_pair, n_col),
        out_shape=jax.ShapeDtypeStruct((rows, int_cols), F32),
        in_specs=[scalar, scalar, scalar, any_space, any_space],
        out_specs=pl.BlockSpec(memory_space=pltpu.VMEM),
        scratch_shapes=scratch,
        compiler_params=pltpu.CompilerParams(
            collective_id=0, has_side_effects=True, vmem_limit_bytes=held + (6 << 20)
        ),
        cost_estimate=pl.CostEstimate(
            flops=6 * rows * depth * n_col * int_cols,
            bytes_accessed=4 * rows * (2 * depth + int_cols),
            transcendentals=0,
        ),
        name="ladder",
    )(amp_tiles.reshape(live), amp_count.reshape(1), int_mask, amplitudes, integrals)


def solution(mesh):
    return jax.shard_map(
        functools.partial(local, mesh.shape["pair"], mesh.shape["col"]),
        mesh=mesh,
        in_specs=(
            P("pair", "col"),
            P("pair", "col"),
            P("pair", "col", None),
            P("pair", "col"),
            P("pair", "col"),
        ),
        out_specs=P("pair", "col"),
        check_vma=False,
    )
```

```python
import functools

import jax
import jax.numpy as jnp
from jax import lax
from jax.experimental import pallas as pl
from jax.experimental.pallas import tpu as pltpu
from jax.sharding import PartitionSpec as P

TILE = 128
CORES = 2
VMEM_BYTES = 60 << 20
MESH = pl.DeviceIdType.MESH
BF16 = jnp.bfloat16
F32 = jnp.float32


def split(value):
    high = value.astype(BF16)
    return high, (value - high.astype(F32)).astype(BF16)


def when(*conditions):
    together = conditions[0]
    for condition in conditions[1:]:
        together = jnp.logical_and(together, condition)
    return pl.when(together)


def kernel(
    n_pair, n_col, list_hbm, count_hbm, mask_hbm, amp_hbm, int_hbm, out_ref,
    list_ref, count_ref, mask_ref, amp, packed, slots, ints, a_high, a_low, b_high, b_low,
    load_small, load_amp, load_int, amp_recv, amp_send, slot_recv, slot_send, int_recv, int_send,
):
    live = packed.shape[1]
    rows, depth = amp.shape
    tile_cols = depth // TILE
    tiles = (rows // TILE) * tile_cols
    int_rows, int_cols = ints.shape[1:]
    half = int_rows // 2
    piece = TILE
    pieces = half // piece

    pair, col = lax.axis_index("pair"), lax.axis_index("col")
    line, line_at, core = n_col // CORES, col // CORES, col % CORES
    wide = n_pair // 2
    high_at, low_at = pair // wide, pair % wide

    sibling = {"col": line_at * CORES + 1 - core}
    above, below = {"col": col + CORES}, {"col": col - CORES}
    across = {"pair": (1 - high_at) * wide + low_at}
    right, left = {"pair": pair + 1}, {"pair": pair - 1}
    has_above, has_below = line_at < line - 1, line_at > 0
    has_right, has_left = low_at < wide - 1, low_at > 0

    int_loads = [
        pltpu.make_async_copy(
            int_hbm.at[pl.ds(at * piece, piece)],
            ints.at[pair, pl.ds(at * piece, piece)],
            load_int.at[at],
        )
        for at in range(2 * pieces)
    ]
    small_loads = [
        pltpu.make_async_copy(source, target, load_small.at[at])
        for at, (source, target) in enumerate(
            ((list_hbm, list_ref), (count_hbm, count_ref), (mask_hbm, mask_ref))
        )
    ]
    amp_load = pltpu.make_async_copy(amp_hbm, amp, load_amp)
    for load in small_loads:
        load.start()
    amp_load.start()
    for load in int_loads:
        load.start()

    barrier = pltpu.get_barrier_semaphore()
    partners = (
        (sibling, None), (across, None), (above, has_above), (below, has_below),
        (right, has_right), (left, has_left),
    )
    for partner, exists in partners:
        def greet(partner=partner):
            pl.semaphore_signal(barrier, inc=1, device_id=partner, device_id_type=MESH)
        if exists is None:
            greet()
        else:
            pl.when(exists)(greet)
    def amp_copy(source, slot, way, target):
        ref = packed.at[source, slot]
        return pltpu.make_async_remote_copy(
            src_ref=ref, dst_ref=ref,
            send_sem=amp_send.at[way, source, slot], recv_sem=amp_recv.at[source, slot],
            device_id=target, device_id_type=MESH,
        )

    def slot_copy(source, way, target):
        ref = slots.at[source]
        return pltpu.make_async_remote_copy(
            src_ref=ref, dst_ref=ref,
            send_sem=slot_send.at[way, source], recv_sem=slot_recv.at[source],
            device_id=target, device_id_type=MESH,
        )

    def int_copy(source, at, way, target):
        ref = ints.at[source, pl.ds(at * piece, piece)]
        return pltpu.make_async_remote_copy(
            src_ref=ref, dst_ref=ref,
            send_sem=int_send.at[way, source, at], recv_sem=int_recv.at[source, at],
            device_id=target, device_id_type=MESH,
        )

    out_ref[...] = jnp.zeros_like(out_ref)
    for load in small_loads:
        load.wait()
    numbers = [
        jnp.where(
            jnp.full((1, TILE), count_ref[0, 0], jnp.int32) > s,
            jnp.full((1, TILE), list_ref[0, 0, s], jnp.int32),
            -1,
        )
        for s in range(live)
    ]
    for t in range(tiles):
        place = jnp.full((1, TILE), -1, jnp.int32)
        for s in range(live):
            place = jnp.where(numbers[s] == t, s, place)
        slots[col, pl.ds(t, 1), :] = place
    amp_load.wait()
    for s in range(live):
        number = jnp.broadcast_to(numbers[s], (TILE, TILE))
        value = jnp.zeros((TILE, TILE), F32)
        for t in range(tiles):
            at = (pl.ds(t // tile_cols * TILE, TILE), pl.ds(t % tile_cols * TILE, TILE))
            value = jnp.where(number == t, amp[at], value)
        packed[col, s] = value

    for at in range(2 * pieces):
        int_loads[at].wait()
        span = pl.ds(at * piece, piece)
        for c in range(int_cols // TILE):
            keep = mask_ref[c, at * piece // TILE].astype(F32)
            cols = pl.ds(c * TILE, TILE)
            ints[pair, span, cols] = ints[pair, span, cols] * keep

    peers = 2
    for _, exists in partners[2:]:
        peers += jnp.where(exists, 1, 0)
    pl.semaphore_wait(barrier, peers)

    def send_own_amp(copy):
        pl.when(has_above)(lambda: copy(0, above).start())
        pl.when(has_below)(lambda: copy(1, below).start())
        copy(2, sibling).start()

    def send_row(source, at):
        pl.when(has_right)(lambda: int_copy(source, at, 0, right).start())
        pl.when(has_left)(lambda: int_copy(source, at, 1, left).start())

    send_own_amp(lambda way, target: slot_copy(col, way, target))
    for s in range(max(live, pieces)):
        if s < live:
            send_own_amp(lambda way, target, s=s: amp_copy(col, s, way, target))
        if s < pieces:
            send_row(pair, s)
            int_copy(pair, pieces + s, 2, across).start()
    for u in range(pieces):
        send_row(pair, pieces + u)
        int_copy(pair, u, 2, across).start()

    def amp_slot(source):
        return jnp.abs(source // CORES - line_at)

    def int_slot(source, part):
        away = jnp.abs(source % wide - low_at)
        same = source // wide == high_at
        near = jnp.where(part == 0, away, jnp.where(away > 0, away + 1, 0))
        far = jnp.where(part == 0, away + 2, jnp.where(away > 0, away + 2, 1))
        return jnp.where(same, near, far)

    def step(now, _):
        def pass_amp(source, exists, way, target, more):
            @when(now >= 1, exists)
            def _():
                slot_copy(source, way, target).wait_recv()
                pl.when(more)(lambda: slot_copy(source, way, target).start())
                slot_copy(source, 2, sibling).start()

        def pass_tile(source, s, exists, way, target, more):
            @when(now >= 1, exists)
            def _():
                amp_copy(source, s, way, target).wait_recv()
                pl.when(more)(lambda: amp_copy(source, s, way, target).start())
                amp_copy(source, s, 2, sibling).start()

        def pass_row(source, at, away, across_too):
            def one(side, exists, way, target, more):
                origin = source + side * away

                @when(away >= 1, exists)
                def _():
                    int_copy(origin, at, way, target).wait_recv()
                    pl.when(more)(lambda: int_copy(origin, at, way, target).start())
                    if across_too:
                        int_copy(origin, at, 2, across).start()

            one(-1, low_at - away >= 0, 0, right, has_right)
            one(1, low_at + away < wide, 1, left, has_left)

        lower, upper = col - CORES * now, col + CORES * now
        pass_amp(lower, line_at - now >= 0, 0, above, has_above)
        pass_amp(upper, line_at + now < line, 1, below, has_below)
        other = (1 - high_at) * wide + low_at
        for s in range(max(live, pieces)):
            if s < live:
                pass_tile(lower, s, line_at - now >= 0, 0, above, has_above)
                pass_tile(upper, s, line_at + now < line, 1, below, has_below)
            if s < pieces:
                pass_row(pair, s, now, True)

                @when(now == 1)
                def _(s=s):
                    int_copy(other, pieces + s, 2, across).wait_recv()
                    send_row(other, pieces + s)

        for u in range(pieces):
            pass_row(pair, pieces + u, now - 1, False)
            pass_row(other, pieces + u, now - 2, False)
            away = now - 2
            pl.when(away == 0)(lambda u=u: int_copy(other, u, 2, across).wait_recv())
            for side, exists in ((-1, low_at - away >= 0), (1, low_at + away < wide)):
                @when(away >= 1, exists)
                def _(side=side, u=u, away=away):
                    int_copy(other + side * away, u, 2, across).wait_recv()

        def from_sibling(source):
            slot_copy(source, 2, sibling).wait_recv()
            for s in range(live):
                amp_copy(source, s, 2, sibling).wait_recv()

        @pl.loop(0, n_pair * 2)
        def _(block):
            source, part = block // 2, block % 2

            @pl.when(int_slot(source, part) == now)
            def _():
                span = pl.ds(pl.multiple_of(part * half, half), half)
                value = ints[source, span]
                b_high[source, span], b_low[source, span] = split(value)

        mate = line_at * CORES + 1 - core

        @pl.loop(0, CORES)
        def _(turn):
            @pl.when(turn == 1)
            def _():
                pl.when(line_at - now >= 0)(lambda: from_sibling(mate - CORES * now))
                when(now >= 1, line_at + now < line)(lambda: from_sibling(mate + CORES * now))

            @pl.loop(0, line)
            def _(place_at):
                source = place_at * CORES + (core + turn) % CORES

                @pl.when(amp_slot(source) == now)
                def _():
                    for t in range(tiles):
                        place = jnp.broadcast_to(slots[source, pl.ds(t, 1), :], (TILE, TILE))
                        value = jnp.zeros((TILE, TILE), F32)
                        for s in range(live):
                            value = jnp.where(place == s, packed[source, s], value)
                        at = (
                            pl.ds(t // tile_cols * TILE, TILE),
                            pl.ds(t % tile_cols * TILE, TILE),
                        )
                        a_high[(source, *at)], a_low[(source, *at)] = split(value)

                start = source * depth
                origin, offset = start // int_rows, start % int_rows
                due = jnp.maximum(amp_slot(source), int_slot(origin, offset // half))

                @pl.when(due == now)
                def _():
                    span = pl.ds(pl.multiple_of(offset, depth), depth)
                    high, low = b_high[origin, span], b_low[origin, span]
                    first = a_high[source]
                    total = jnp.dot(first, high, preferred_element_type=F32)
                    total += jnp.dot(first, low, preferred_element_type=F32)
                    total += jnp.dot(a_low[source], high, preferred_element_type=F32)
                    out_ref[...] += total

        return 0

    steps = max(line - 1, wide + 1)
    lax.fori_loop(0, steps + 1, step, 0)

    @pl.loop(0, n_col)
    def _(source):
        mine = source % CORES == core
        at = source // CORES

        def drain(way, target):
            slot_copy(source, way, target).wait_send()
            for s in range(live):
                amp_copy(source, s, way, target).wait_send()

        when(mine, at <= line_at, has_above)(lambda: drain(0, above))
        when(mine, at >= line_at, has_below)(lambda: drain(1, below))
        pl.when(mine)(lambda: drain(2, sibling))

    @pl.loop(0, n_pair)
    def _(source):
        same = source // wide == high_at
        at = source % wide

        def drain(first, way, target):
            for u in range(pieces):
                int_copy(source, first + u, way, target).wait_send()

        when(same, at <= low_at, has_right)(lambda: drain(0, 0, right))
        when(same, at >= low_at, has_left)(lambda: drain(0, 1, left))
        pl.when(same)(lambda: drain(0, 2, across))
        when(at <= low_at, has_right)(lambda: drain(pieces, 0, right))
        when(at >= low_at, has_left)(lambda: drain(pieces, 1, left))
        pl.when(source == pair)(lambda: drain(pieces, 2, across))


def local(n_pair, n_col, amplitudes, integrals, amp_tiles, amp_count, int_mask):
    rows, depth = amplitudes.shape
    int_rows, int_cols = integrals.shape
    live = amp_tiles.shape[-1]
    tiles = (rows // TILE) * (depth // TILE)
    half = int_rows // 2
    assert n_pair % 2 == 0 and n_col % CORES == 0
    assert half % depth == 0 and half % TILE == 0
    pieces = int_rows // TILE
    scratch = [
        pltpu.SMEM(amp_tiles.shape, jnp.int32),
        pltpu.SMEM(amp_count.shape, jnp.int32),
        pltpu.SMEM(int_mask.shape[::-1], jnp.int32),
        pltpu.VMEM((rows, depth), F32),
        pltpu.VMEM((n_col, live, TILE, TILE), F32),
        pltpu.VMEM((n_col, tiles, TILE), jnp.int32),
        pltpu.VMEM((n_pair, int_rows, int_cols), F32),
        pltpu.VMEM((n_col, rows, depth), BF16),
        pltpu.VMEM((n_col, rows, depth), BF16),
        pltpu.VMEM((n_pair, int_rows, int_cols), BF16),
        pltpu.VMEM((n_pair, int_rows, int_cols), BF16),
        pltpu.SemaphoreType.DMA((3,)),
        pltpu.SemaphoreType.DMA,
        pltpu.SemaphoreType.DMA((pieces,)),
        pltpu.SemaphoreType.DMA((n_col, live)),
        pltpu.SemaphoreType.DMA((3, n_col, live)),
        pltpu.SemaphoreType.DMA((n_col,)),
        pltpu.SemaphoreType.DMA((3, n_col)),
        pltpu.SemaphoreType.DMA((n_pair, pieces)),
        pltpu.SemaphoreType.DMA((3, n_pair, pieces)),
    ]
    return pl.pallas_call(
        functools.partial(kernel, n_pair, n_col),
        out_shape=jax.ShapeDtypeStruct((rows, int_cols), F32),
        in_specs=[pl.BlockSpec(memory_space=pltpu.HBM)] * 5,
        out_specs=pl.BlockSpec(memory_space=pltpu.VMEM),
        scratch_shapes=scratch,
        compiler_params=pltpu.CompilerParams(
            collective_id=0, has_side_effects=True, vmem_limit_bytes=VMEM_BYTES
        ),
        cost_estimate=pl.CostEstimate(
            flops=6 * rows * depth * n_col * int_cols,
            bytes_accessed=4 * rows * (2 * depth + int_cols),
            transcendentals=0,
        ),
        name="ladder",
    )(amp_tiles, amp_count, int_mask.T, amplitudes, integrals)


def solution(mesh):
    return jax.shard_map(
        functools.partial(local, mesh.shape["pair"], mesh.shape["col"]),
        mesh=mesh,
        in_specs=(
            P("pair", "col"),
            P("pair", "col"),
            P("pair", "col", None),
            P("pair", "col"),
            P("pair", "col"),
        ),
        out_specs=P("pair", "col"),
        check_vma=False,
    )
```

```python
import functools

import jax
import jax.numpy as jnp
from jax import lax
from jax.experimental import pallas as pl
from jax.experimental.pallas import tpu as pltpu
from jax.sharding import PartitionSpec as P

TILE = 128
CORES = 2
VMEM_BYTES = 60 << 20
MESH = pl.DeviceIdType.MESH
BF16 = jnp.bfloat16
F32 = jnp.float32


def split(value):
    high = value.astype(BF16)
    return high, (value - high.astype(F32)).astype(BF16)


def when(*conditions):
    if any(condition is False for condition in conditions):
        return lambda body: None
    traced = [condition for condition in conditions if condition is not True]
    if not traced:
        return lambda body: body()
    return pl.when(functools.reduce(jnp.logical_and, traced))


def kernel(
    n_pair, n_col, list_hbm, count_hbm, mask_hbm, amp_hbm, int_hbm, out_ref,
    list_ref, count_ref, mask_ref, amp, packed, slots, ints, a_high, a_low, b_high, b_low,
    load_small, load_amp, load_int, amp_recv, amp_send, slot_recv, slot_send, int_recv, int_send,
):
    live = packed.shape[1]
    rows, depth = amp.shape
    tile_cols = depth // TILE
    tiles = (rows // TILE) * tile_cols
    int_rows, int_cols = ints.shape[1:]
    half = int_rows // 2
    piece = TILE
    pieces = half // piece

    pair, col = lax.axis_index("pair"), lax.axis_index("col")
    line, line_at, core = n_col // CORES, col // CORES, col % CORES
    wide = n_pair // 2
    high_at, low_at = pair // wide, pair % wide

    sibling = {"col": line_at * CORES + 1 - core}
    above, below = {"col": col + CORES}, {"col": col - CORES}
    across = {"pair": (1 - high_at) * wide + low_at}
    right, left = {"pair": pair + 1}, {"pair": pair - 1}
    has_above, has_below = line_at < line - 1, line_at > 0
    has_right, has_left = low_at < wide - 1, low_at > 0
    far = {"col": (line - 1 - line_at) * CORES + core}
    is_end = (line_at == 0) | (line_at == line - 1) if line > 2 else False
    passes_up = (line_at < line - 2) if line > 2 else has_above
    passes_down = (line_at > 1) if line > 2 else has_below

    int_loads = [
        pltpu.make_async_copy(
            int_hbm.at[pl.ds(at * piece, piece)],
            ints.at[pair, pl.ds(at * piece, piece)],
            load_int.at[at],
        )
        for at in range(2 * pieces)
    ]
    small_loads = [
        pltpu.make_async_copy(source, target, load_small.at[at])
        for at, (source, target) in enumerate(
            ((list_hbm, list_ref), (count_hbm, count_ref), (mask_hbm, mask_ref))
        )
    ]
    amp_load = pltpu.make_async_copy(amp_hbm, amp, load_amp)
    for load in small_loads:
        load.start()
    amp_load.start()
    for load in int_loads:
        load.start()

    barrier = pltpu.get_barrier_semaphore()
    partners = (
        (sibling, None), (across, None), (above, has_above), (below, has_below),
        (right, has_right), (left, has_left), (far, is_end),
    )
    for partner, exists in partners:
        def greet(partner=partner):
            pl.semaphore_signal(barrier, inc=1, device_id=partner, device_id_type=MESH)
        when(exists is None or exists)(greet)
    def amp_copy(source, slot, way, target):
        ref = packed.at[source, slot]
        return pltpu.make_async_remote_copy(
            src_ref=ref, dst_ref=ref,
            send_sem=amp_send.at[way, source, slot], recv_sem=amp_recv.at[source, slot],
            device_id=target, device_id_type=MESH,
        )

    def slot_copy(source, way, target):
        ref = slots.at[source]
        return pltpu.make_async_remote_copy(
            src_ref=ref, dst_ref=ref,
            send_sem=slot_send.at[way, source], recv_sem=slot_recv.at[source],
            device_id=target, device_id_type=MESH,
        )

    def int_copy(source, at, way, target):
        ref = ints.at[source, pl.ds(at * piece, piece)]
        return pltpu.make_async_remote_copy(
            src_ref=ref, dst_ref=ref,
            send_sem=int_send.at[way, source, at], recv_sem=int_recv.at[source, at],
            device_id=target, device_id_type=MESH,
        )

    out_ref[...] = jnp.zeros_like(out_ref)
    for load in small_loads:
        load.wait()
    numbers = [
        jnp.where(
            jnp.full((1, TILE), count_ref[0, 0], jnp.int32) > s,
            jnp.full((1, TILE), list_ref[0, 0, s], jnp.int32),
            -1,
        )
        for s in range(live)
    ]
    for t in range(tiles):
        place = jnp.full((1, TILE), -1, jnp.int32)
        for s in range(live):
            place = jnp.where(numbers[s] == t, s, place)
        slots[col, pl.ds(t, 1), :] = place
    amp_load.wait()
    for s in range(live):
        number = jnp.broadcast_to(numbers[s], (TILE, TILE))
        value = jnp.zeros((TILE, TILE), F32)
        for t in range(tiles):
            at = (pl.ds(t // tile_cols * TILE, TILE), pl.ds(t % tile_cols * TILE, TILE))
            value = jnp.where(number == t, amp[at], value)
        packed[col, s] = value

    for at in range(2 * pieces):
        int_loads[at].wait()
        span = pl.ds(at * piece, piece)
        for c in range(int_cols // TILE):
            keep = mask_ref[c, at * piece // TILE].astype(F32)
            cols = pl.ds(c * TILE, TILE)
            ints[pair, span, cols] = ints[pair, span, cols] * keep

    peers = 2
    for _, exists in partners[2:]:
        if exists is not False:
            peers += jnp.where(exists, 1, 0)
    pl.semaphore_wait(barrier, peers)

    def send_own_amp(copy):
        pl.when(has_above)(lambda: copy(0, above).start())
        pl.when(has_below)(lambda: copy(1, below).start())
        when(is_end)(lambda: copy(3, far).start())
        copy(2, sibling).start()

    def send_row(source, at):
        pl.when(has_right)(lambda: int_copy(source, at, 0, right).start())
        pl.when(has_left)(lambda: int_copy(source, at, 1, left).start())

    send_own_amp(lambda way, target: slot_copy(col, way, target))
    for s in range(max(live, pieces)):
        if s < live:
            send_own_amp(lambda way, target, s=s: amp_copy(col, s, way, target))
        if s < pieces:
            send_row(pair, s)
            int_copy(pair, pieces + s, 2, across).start()
    for u in range(pieces):
        send_row(pair, pieces + u)
        int_copy(pair, u, 2, across).start()

    def amp_slot(source):
        return jnp.abs(source // CORES - line_at)

    def int_slot(source, part):
        away = jnp.abs(source % wide - low_at)
        same = source // wide == high_at
        near = jnp.where(part == 0, away, jnp.where(away > 0, away + 1, 0))
        far = jnp.where(part == 0, away + 2, jnp.where(away > 0, away + 2, 1))
        return jnp.where(same, near, far)

    def step(now):
        def pass_amp(source, exists, way, target, more):
            @when(now >= 1, now < line, exists)
            def _():
                slot_copy(source, way, target).wait_recv()
                when(more)(lambda: slot_copy(source, way, target).start())
                slot_copy(source, 2, sibling).start()

        def pass_tile(source, s, exists, way, target, more):
            @when(now >= 1, now < line, exists)
            def _():
                amp_copy(source, s, way, target).wait_recv()
                when(more)(lambda: amp_copy(source, s, way, target).start())
                amp_copy(source, s, 2, sibling).start()

        def pass_row(source, at, away, across_too):
            def one(side, exists, way, target, more):
                origin = source + side * away

                @when(away >= 1, away < wide, exists)
                def _():
                    int_copy(origin, at, way, target).wait_recv()
                    pl.when(more)(lambda: int_copy(origin, at, way, target).start())
                    if across_too:
                        int_copy(origin, at, 2, across).start()

            one(-1, low_at - away >= 0, 0, right, has_right)
            one(1, low_at + away < wide, 1, left, has_left)

        lower, upper = col - CORES * now, col + CORES * now
        more_above = has_above if line == 2 else has_above & ((line_at != now) | passes_up)
        more_below = has_below if line == 2 else has_below & (
            (line_at + now != line - 1) | passes_down
        )
        pass_amp(lower, line_at - now >= 0, 0, above, more_above)
        pass_amp(upper, line_at + now < line, 1, below, more_below)
        other = (1 - high_at) * wide + low_at
        for s in range(max(live, pieces)):
            if s < live:
                pass_tile(lower, s, line_at - now >= 0, 0, above, more_above)
                pass_tile(upper, s, line_at + now < line, 1, below, more_below)
            if s < pieces:
                pass_row(pair, s, now, True)

                @when(now == 1)
                def _(s=s):
                    int_copy(other, pieces + s, 2, across).wait_recv()
                    send_row(other, pieces + s)

        for u in range(pieces):
            pass_row(pair, pieces + u, now - 1, False)
            pass_row(other, pieces + u, now - 2, False)
            away = now - 2
            when(away == 0)(lambda u=u: int_copy(other, u, 2, across).wait_recv())
            for side, exists in ((-1, low_at - away >= 0), (1, low_at + away < wide)):
                @when(away >= 1, away < wide, exists)
                def _(side=side, u=u, away=away):
                    int_copy(other + side * away, u, 2, across).wait_recv()

        def from_sibling(source):
            slot_copy(source, 2, sibling).wait_recv()
            for s in range(live):
                amp_copy(source, s, 2, sibling).wait_recv()

        @pl.loop(0, n_pair * 2)
        def _(block):
            source, part = block // 2, block % 2

            @pl.when(int_slot(source, part) == now)
            def _():
                span = pl.ds(pl.multiple_of(part * half, half), half)
                value = ints[source, span]
                b_high[source, span], b_low[source, span] = split(value)

        mate = line_at * CORES + 1 - core

        @pl.loop(0, CORES)
        def _(turn):
            @pl.when(turn == 1)
            def _():
                when(line_at - now >= 0)(lambda: from_sibling(mate - CORES * now))
                when(now >= 1, now < line, line_at + now < line)(lambda: from_sibling(mate + CORES * now))

            @pl.loop(0, line)
            def _(place_at):
                source = place_at * CORES + (core + turn) % CORES

                @pl.when(amp_slot(source) == now)
                def _():
                    for t in range(tiles):
                        place = jnp.broadcast_to(slots[source, pl.ds(t, 1), :], (TILE, TILE))
                        value = jnp.zeros((TILE, TILE), F32)
                        for s in range(live):
                            value = jnp.where(place == s, packed[source, s], value)
                        at = (
                            pl.ds(t // tile_cols * TILE, TILE),
                            pl.ds(t % tile_cols * TILE, TILE),
                        )
                        a_high[(source, *at)], a_low[(source, *at)] = split(value)

                start = source * depth
                origin, offset = start // int_rows, start % int_rows
                due = jnp.maximum(amp_slot(source), int_slot(origin, offset // half))

                @pl.when(due == now)
                def _():
                    span = pl.ds(pl.multiple_of(offset, depth), depth)
                    high, low = b_high[origin, span], b_low[origin, span]
                    first = a_high[source]
                    total = jnp.dot(first, high, preferred_element_type=F32)
                    total += jnp.dot(first, low, preferred_element_type=F32)
                    total += jnp.dot(a_low[source], high, preferred_element_type=F32)
                    out_ref[...] += total

    for now in range(max(line - 1, wide + 1) + 1):
        step(now)

    @pl.loop(0, n_col)
    def _(source):
        mine = source % CORES == core
        at = source // CORES

        def drain(way, target):
            slot_copy(source, way, target).wait_send()
            for s in range(live):
                amp_copy(source, s, way, target).wait_send()

        up, down = at <= line_at, at >= line_at
        if line > 2:
            up &= (at > 0) | (line_at != line - 2)
            down &= (at < line - 1) | (line_at != 1)
        when(mine, up, has_above)(lambda: drain(0, above))
        when(mine, down, has_below)(lambda: drain(1, below))
        when(mine, at == line_at, is_end)(lambda: drain(3, far))
        pl.when(mine)(lambda: drain(2, sibling))

    @pl.loop(0, n_pair)
    def _(source):
        same = source // wide == high_at
        at = source % wide

        def drain(first, way, target):
            for u in range(pieces):
                int_copy(source, first + u, way, target).wait_send()

        when(same, at <= low_at, has_right)(lambda: drain(0, 0, right))
        when(same, at >= low_at, has_left)(lambda: drain(0, 1, left))
        pl.when(same)(lambda: drain(0, 2, across))
        when(at <= low_at, has_right)(lambda: drain(pieces, 0, right))
        when(at >= low_at, has_left)(lambda: drain(pieces, 1, left))
        pl.when(source == pair)(lambda: drain(pieces, 2, across))


def local(n_pair, n_col, amplitudes, integrals, amp_tiles, amp_count, int_mask):
    rows, depth = amplitudes.shape
    int_rows, int_cols = integrals.shape
    live = amp_tiles.shape[-1]
    tiles = (rows // TILE) * (depth // TILE)
    half = int_rows // 2
    assert n_pair % 2 == 0 and n_col % CORES == 0
    assert half % depth == 0 and half % TILE == 0
    pieces = int_rows // TILE
    scratch = [
        pltpu.SMEM(amp_tiles.shape, jnp.int32),
        pltpu.SMEM(amp_count.shape, jnp.int32),
        pltpu.SMEM(int_mask.shape[::-1], jnp.int32),
        pltpu.VMEM((rows, depth), F32),
        pltpu.VMEM((n_col, live, TILE, TILE), F32),
        pltpu.VMEM((n_col, tiles, TILE), jnp.int32),
        pltpu.VMEM((n_pair, int_rows, int_cols), F32),
        pltpu.VMEM((n_col, rows, depth), BF16),
        pltpu.VMEM((n_col, rows, depth), BF16),
        pltpu.VMEM((n_pair, int_rows, int_cols), BF16),
        pltpu.VMEM((n_pair, int_rows, int_cols), BF16),
        pltpu.SemaphoreType.DMA((3,)),
        pltpu.SemaphoreType.DMA,
        pltpu.SemaphoreType.DMA((pieces,)),
        pltpu.SemaphoreType.DMA((n_col, live)),
        pltpu.SemaphoreType.DMA((4, n_col, live)),
        pltpu.SemaphoreType.DMA((n_col,)),
        pltpu.SemaphoreType.DMA((4, n_col)),
        pltpu.SemaphoreType.DMA((n_pair, pieces)),
        pltpu.SemaphoreType.DMA((3, n_pair, pieces)),
    ]
    return pl.pallas_call(
        functools.partial(kernel, n_pair, n_col),
        out_shape=pltpu.VMEM((rows, int_cols), F32),
        in_specs=[pl.BlockSpec(memory_space=pltpu.HBM)] * 5,
        out_specs=pl.BlockSpec(memory_space=pltpu.VMEM),
        scratch_shapes=scratch,
        compiler_params=pltpu.CompilerParams(
            collective_id=0, has_side_effects=True, vmem_limit_bytes=VMEM_BYTES
        ),
        cost_estimate=pl.CostEstimate(
            flops=6 * rows * depth * n_col * int_cols,
            bytes_accessed=4 * rows * (2 * depth + int_cols),
            transcendentals=0,
        ),
        name="ladder",
    )(amp_tiles, amp_count, int_mask.T, amplitudes, integrals)


def solution(mesh):
    return jax.shard_map(
        functools.partial(local, mesh.shape["pair"], mesh.shape["col"]),
        mesh=mesh,
        in_specs=(
            P("pair", "col"),
            P("pair", "col"),
            P("pair", "col", None),
            P("pair", "col"),
            P("pair", "col"),
        ),
        out_specs=P("pair", "col"),
        check_vma=False,
    )
```

```python
import functools

import jax
import jax.numpy as jnp
from jax import lax
from jax.experimental import pallas as pl
from jax.experimental.pallas import tpu as pltpu
from jax.sharding import PartitionSpec as P

TILE = 128
CORES = 2
VMEM_BYTES = 60 << 20
MESH = pl.DeviceIdType.MESH
BF16 = jnp.bfloat16
F32 = jnp.float32


def split(value):
    high = value.astype(BF16)
    return high, (value - high.astype(F32)).astype(BF16)


def when(*conditions):
    together = conditions[0]
    for condition in conditions[1:]:
        together = jnp.logical_and(together, condition)
    return pl.when(together)


def kernel(
    n_pair, n_col, list_hbm, count_hbm, mask_hbm, amp_hbm, int_hbm, out_ref,
    list_ref, count_ref, mask_ref, place_ref, amp, part_high, part_low, packed, slots, ints, a_high, a_low, b_high, b_low,
    load_small, load_amp, load_int, load_place, amp_recv, amp_send, slot_recv, slot_send, int_recv, int_send,
):
    live = packed.shape[1]
    rows, depth = a_high.shape[1:]
    tile_cols = depth // TILE
    tiles = amp.shape[0]
    int_rows, int_cols = ints.shape[1:]
    half = int_rows // 2
    piece = TILE
    pieces = half // piece

    pair, col = lax.axis_index("pair"), lax.axis_index("col")
    line, line_at, core = n_col // CORES, col // CORES, col % CORES
    wide = n_pair // 2
    high_at, low_at = pair // wide, pair % wide

    sibling = {"col": line_at * CORES + 1 - core}
    above, below = {"col": col + CORES}, {"col": col - CORES}
    across = {"pair": (1 - high_at) * wide + low_at}
    right, left = {"pair": pair + 1}, {"pair": pair - 1}
    has_above, has_below = line_at < line - 1, line_at > 0
    has_right, has_left = low_at < wide - 1, low_at > 0

    int_loads = [
        pltpu.make_async_copy(
            int_hbm.at[pl.ds(at * piece, piece)],
            ints.at[pair, pl.ds(at * piece, piece)],
            load_int.at[at],
        )
        for at in range(2 * pieces)
    ]
    small_loads = [
        pltpu.make_async_copy(source, target, load_small.at[at])
        for at, (source, target) in enumerate(
            ((list_hbm, list_ref), (count_hbm, count_ref), (mask_hbm, mask_ref))
        )
    ]
    def tile_at(t):
        return pl.ds(t // tile_cols * TILE, TILE), pl.ds(t % tile_cols * TILE, TILE)

    amp_loads = [
        pltpu.make_async_copy(amp_hbm.at[tile_at(t)], amp.at[t], load_amp.at[t])
        for t in range(tiles)
    ]
    for load in small_loads:
        load.start()
    for load in amp_loads:
        load.start()
    for load in int_loads:
        load.start()

    barrier = pltpu.get_barrier_semaphore()
    partners = (
        (sibling, None), (across, None), (above, has_above), (below, has_below),
        (right, has_right), (left, has_left),
    )
    for partner, exists in partners:
        def greet(partner=partner):
            pl.semaphore_signal(barrier, inc=1, device_id=partner, device_id_type=MESH)
        if exists is None:
            greet()
        else:
            pl.when(exists)(greet)
    def amp_copy(source, slot, way, target):
        ref = packed.at[source, slot]
        return pltpu.make_async_remote_copy(
            src_ref=ref, dst_ref=ref,
            send_sem=amp_send.at[way, source, slot], recv_sem=amp_recv.at[source, slot],
            device_id=target, device_id_type=MESH,
        )

    def slot_copy(source, way, target):
        ref = slots.at[source]
        return pltpu.make_async_remote_copy(
            src_ref=ref, dst_ref=ref,
            send_sem=slot_send.at[way, source], recv_sem=slot_recv.at[source],
            device_id=target, device_id_type=MESH,
        )

    def int_copy(source, at, way, target):
        ref = ints.at[source, pl.ds(at * piece, piece)]
        return pltpu.make_async_remote_copy(
            src_ref=ref, dst_ref=ref,
            send_sem=int_send.at[way, source, at], recv_sem=int_recv.at[source, at],
            device_id=target, device_id_type=MESH,
        )

    def place_copy(source):
        return pltpu.make_async_copy(
            slots.at[source], place_ref.at[source], load_place.at[source]
        )

    out_ref[...] = jnp.zeros_like(out_ref)
    part_high[live] = jnp.zeros((TILE, TILE), BF16)
    part_low[live] = jnp.zeros((TILE, TILE), BF16)
    for load in small_loads:
        load.wait()
    numbers = [
        jnp.where(
            jnp.full((1, TILE), count_ref[0, 0], jnp.int32) > s,
            jnp.full((1, TILE), list_ref[0, 0, s], jnp.int32),
            -1,
        )
        for s in range(live)
    ]
    for t in range(tiles):
        place = jnp.full((1, TILE), live, jnp.int32)
        for s in range(live):
            place = jnp.where(numbers[s] == t, s, place)
        slots[col, pl.ds(t, 1), :] = place
    place_copy(col).start()
    for load in amp_loads:
        load.wait()
    for s in range(live):
        packed[col, s] = amp[list_ref[0, 0, s]]

    for at in range(2 * pieces):
        int_loads[at].wait()
        span = pl.ds(at * piece, piece)
        for c in range(int_cols // TILE):
            keep = mask_ref[c, at * piece // TILE].astype(F32)
            cols = pl.ds(c * TILE, TILE)
            ints[pair, span, cols] = ints[pair, span, cols] * keep

    peers = 2
    for _, exists in partners[2:]:
        peers += jnp.where(exists, 1, 0)
    pl.semaphore_wait(barrier, peers)

    def send_own_amp(copy):
        pl.when(has_above)(lambda: copy(0, above).start())
        pl.when(has_below)(lambda: copy(1, below).start())
        copy(2, sibling).start()

    def send_row(source, at):
        pl.when(has_right)(lambda: int_copy(source, at, 0, right).start())
        pl.when(has_left)(lambda: int_copy(source, at, 1, left).start())

    send_own_amp(lambda way, target: slot_copy(col, way, target))
    for s in range(max(live, pieces)):
        if s < live:
            send_own_amp(lambda way, target, s=s: amp_copy(col, s, way, target))
        if s < pieces:
            send_row(pair, s)
            int_copy(pair, pieces + s, 2, across).start()
    for u in range(pieces):
        send_row(pair, pieces + u)
        int_copy(pair, u, 2, across).start()

    def amp_slot(source):
        return jnp.abs(source // CORES - line_at)

    def int_slot(source, part):
        away = jnp.abs(source % wide - low_at)
        same = source // wide == high_at
        near = jnp.where(part == 0, away, jnp.where(away > 0, away + 1, 0))
        far = jnp.where(part == 0, away + 2, jnp.where(away > 0, away + 2, 1))
        return jnp.where(same, near, far)

    def step(now, _):
        def pass_amp(source, exists, way, target, more):
            @when(now >= 1, exists)
            def _():
                slot_copy(source, way, target).wait_recv()
                place_copy(source).start()
                pl.when(more)(lambda: slot_copy(source, way, target).start())
                slot_copy(source, 2, sibling).start()

        def pass_tile(source, s, exists, way, target, more):
            @when(now >= 1, exists)
            def _():
                amp_copy(source, s, way, target).wait_recv()
                pl.when(more)(lambda: amp_copy(source, s, way, target).start())
                amp_copy(source, s, 2, sibling).start()

        def pass_row(source, at, away, across_too):
            def one(side, exists, way, target, more):
                origin = source + side * away

                @when(away >= 1, exists)
                def _():
                    int_copy(origin, at, way, target).wait_recv()
                    pl.when(more)(lambda: int_copy(origin, at, way, target).start())
                    if across_too:
                        int_copy(origin, at, 2, across).start()

            one(-1, low_at - away >= 0, 0, right, has_right)
            one(1, low_at + away < wide, 1, left, has_left)

        lower, upper = col - CORES * now, col + CORES * now
        pass_amp(lower, line_at - now >= 0, 0, above, has_above)
        pass_amp(upper, line_at + now < line, 1, below, has_below)
        other = (1 - high_at) * wide + low_at
        for s in range(max(live, pieces)):
            if s < live:
                pass_tile(lower, s, line_at - now >= 0, 0, above, has_above)
                pass_tile(upper, s, line_at + now < line, 1, below, has_below)
            if s < pieces:
                pass_row(pair, s, now, True)

                @when(now == 1)
                def _(s=s):
                    int_copy(other, pieces + s, 2, across).wait_recv()
                    send_row(other, pieces + s)

        for u in range(pieces):
            pass_row(pair, pieces + u, now - 1, False)
            pass_row(other, pieces + u, now - 2, False)
            away = now - 2
            pl.when(away == 0)(lambda u=u: int_copy(other, u, 2, across).wait_recv())
            for side, exists in ((-1, low_at - away >= 0), (1, low_at + away < wide)):
                @when(away >= 1, exists)
                def _(side=side, u=u, away=away):
                    int_copy(other + side * away, u, 2, across).wait_recv()

        def from_sibling(source):
            slot_copy(source, 2, sibling).wait_recv()
            place_copy(source).start()
            for s in range(live):
                amp_copy(source, s, 2, sibling).wait_recv()

        @pl.loop(0, n_pair * 2)
        def _(block):
            source, part = block // 2, block % 2

            @pl.when(int_slot(source, part) == now)
            def _():
                span = pl.ds(pl.multiple_of(part * half, half), half)
                value = ints[source, span]
                b_high[source, span], b_low[source, span] = split(value)

        mate = line_at * CORES + 1 - core

        @pl.loop(0, CORES)
        def _(turn):
            @pl.when(turn == 1)
            def _():
                pl.when(line_at - now >= 0)(lambda: from_sibling(mate - CORES * now))
                when(now >= 1, line_at + now < line)(lambda: from_sibling(mate + CORES * now))

            @pl.loop(0, line)
            def _(place_at):
                source = place_at * CORES + (core + turn) % CORES

                @pl.when(amp_slot(source) == now)
                def _():
                    for s in range(live):
                        part_high[s], part_low[s] = split(packed[source, s])
                    place_copy(source).wait()
                    for t in range(tiles):
                        place = place_ref[source, t, 0]
                        a_high[(source, *tile_at(t))] = part_high[place]
                        a_low[(source, *tile_at(t))] = part_low[place]

                start = source * depth
                origin, offset = start // int_rows, start % int_rows
                due = jnp.maximum(amp_slot(source), int_slot(origin, offset // half))

                @pl.when(due == now)
                def _():
                    span = pl.ds(pl.multiple_of(offset, depth), depth)
                    high, low = b_high[origin, span], b_low[origin, span]
                    first = a_high[source]
                    total = jnp.dot(first, high, preferred_element_type=F32)
                    total += jnp.dot(first, low, preferred_element_type=F32)
                    total += jnp.dot(a_low[source], high, preferred_element_type=F32)
                    out_ref[...] += total

        return 0

    steps = max(line - 1, wide + 1)
    lax.fori_loop(0, steps + 1, step, 0)

    @pl.loop(0, n_col)
    def _(source):
        mine = source % CORES == core
        at = source // CORES

        def drain(way, target):
            slot_copy(source, way, target).wait_send()
            for s in range(live):
                amp_copy(source, s, way, target).wait_send()

        when(mine, at <= line_at, has_above)(lambda: drain(0, above))
        when(mine, at >= line_at, has_below)(lambda: drain(1, below))
        pl.when(mine)(lambda: drain(2, sibling))

    @pl.loop(0, n_pair)
    def _(source):
        same = source // wide == high_at
        at = source % wide

        def drain(first, way, target):
            for u in range(pieces):
                int_copy(source, first + u, way, target).wait_send()

        when(same, at <= low_at, has_right)(lambda: drain(0, 0, right))
        when(same, at >= low_at, has_left)(lambda: drain(0, 1, left))
        pl.when(same)(lambda: drain(0, 2, across))
        when(at <= low_at, has_right)(lambda: drain(pieces, 0, right))
        when(at >= low_at, has_left)(lambda: drain(pieces, 1, left))
        pl.when(source == pair)(lambda: drain(pieces, 2, across))


def local(n_pair, n_col, amplitudes, integrals, amp_tiles, amp_count, int_mask):
    rows, depth = amplitudes.shape
    int_rows, int_cols = integrals.shape
    live = amp_tiles.shape[-1]
    tiles = (rows // TILE) * (depth // TILE)
    half = int_rows // 2
    assert n_pair % 2 == 0 and n_col % CORES == 0
    assert half % depth == 0 and half % TILE == 0
    pieces = int_rows // TILE
    scratch = [
        pltpu.SMEM(amp_tiles.shape, jnp.int32),
        pltpu.SMEM(amp_count.shape, jnp.int32),
        pltpu.SMEM(int_mask.shape[::-1], jnp.int32),
        pltpu.SMEM((n_col, tiles, TILE), jnp.int32),
        pltpu.VMEM((tiles, TILE, TILE), F32),
        pltpu.VMEM((live + 1, TILE, TILE), BF16),
        pltpu.VMEM((live + 1, TILE, TILE), BF16),
        pltpu.VMEM((n_col, live, TILE, TILE), F32),
        pltpu.VMEM((n_col, tiles, TILE), jnp.int32),
        pltpu.VMEM((n_pair, int_rows, int_cols), F32),
        pltpu.VMEM((n_col, rows, depth), BF16),
        pltpu.VMEM((n_col, rows, depth), BF16),
        pltpu.VMEM((n_pair, int_rows, int_cols), BF16),
        pltpu.VMEM((n_pair, int_rows, int_cols), BF16),
        pltpu.SemaphoreType.DMA((3,)),
        pltpu.SemaphoreType.DMA((tiles,)),
        pltpu.SemaphoreType.DMA((pieces,)),
        pltpu.SemaphoreType.DMA((n_col,)),
        pltpu.SemaphoreType.DMA((n_col, live)),
        pltpu.SemaphoreType.DMA((3, n_col, live)),
        pltpu.SemaphoreType.DMA((n_col,)),
        pltpu.SemaphoreType.DMA((3, n_col)),
        pltpu.SemaphoreType.DMA((n_pair, pieces)),
        pltpu.SemaphoreType.DMA((3, n_pair, pieces)),
    ]
    return pl.pallas_call(
        functools.partial(kernel, n_pair, n_col),
        out_shape=pltpu.VMEM((rows, int_cols), F32),
        in_specs=[pl.BlockSpec(memory_space=pltpu.HBM)] * 5,
        out_specs=pl.BlockSpec(memory_space=pltpu.VMEM),
        scratch_shapes=scratch,
        compiler_params=pltpu.CompilerParams(
            collective_id=0, has_side_effects=True, vmem_limit_bytes=VMEM_BYTES
        ),
        cost_estimate=pl.CostEstimate(
            flops=6 * rows * depth * n_col * int_cols,
            bytes_accessed=4 * rows * (2 * depth + int_cols),
            transcendentals=0,
        ),
        name="ladder",
    )(amp_tiles, amp_count, int_mask.T, amplitudes, integrals)


def solution(mesh):
    return jax.shard_map(
        functools.partial(local, mesh.shape["pair"], mesh.shape["col"]),
        mesh=mesh,
        in_specs=(
            P("pair", "col"),
            P("pair", "col"),
            P("pair", "col", None),
            P("pair", "col"),
            P("pair", "col"),
        ),
        out_specs=P("pair", "col"),
        check_vma=False,
    )
```

```python
import functools

import jax
import jax.numpy as jnp
from jax import lax
from jax.experimental import pallas as pl
from jax.experimental.pallas import tpu as pltpu
from jax.sharding import PartitionSpec as P

TILE = 128
CORES = 2
VMEM_BYTES = 60 << 20
MESH = pl.DeviceIdType.MESH
BF16 = jnp.bfloat16
F32 = jnp.float32


def split(value):
    high = value.astype(BF16)
    return high, (value - high.astype(F32)).astype(BF16)


def when(*conditions):
    together = conditions[0]
    for condition in conditions[1:]:
        together = jnp.logical_and(together, condition)
    return pl.when(together)


def kernel(
    n_pair, n_col, list_hbm, count_hbm, mask_hbm, amp_hbm, int_hbm, out_ref,
    list_ref, count_ref, mask_ref, place_ref, amp, part_high, part_low, packed, slots, ints, a_high, a_low, b_high, b_low,
    load_small, load_amp, load_int, load_place, amp_recv, amp_send, slot_recv, slot_send, int_recv, int_send,
):
    live = packed.shape[1]
    rows, depth = a_high.shape[1:]
    tile_cols = depth // TILE
    tiles = amp.shape[0]
    int_rows, int_cols = ints.shape[1:]
    half = int_rows // 2
    piece = TILE
    pieces = half // piece

    pair, col = lax.axis_index("pair"), lax.axis_index("col")
    line, line_at, core = n_col // CORES, col // CORES, col % CORES
    wide = n_pair // 2
    high_at, low_at = pair // wide, pair % wide

    sibling = {"col": line_at * CORES + 1 - core}
    above, below = {"col": col + CORES}, {"col": col - CORES}
    across = {"pair": (1 - high_at) * wide + low_at}
    right, left = {"pair": pair + 1}, {"pair": pair - 1}
    has_above, has_below = line_at < line - 1, line_at > 0
    has_right, has_left = low_at < wide - 1, low_at > 0

    int_loads = [
        pltpu.make_async_copy(
            int_hbm.at[pl.ds(at * piece, piece)],
            ints.at[pair, pl.ds(at * piece, piece)],
            load_int.at[at],
        )
        for at in range(2 * pieces)
    ]
    small_loads = [
        pltpu.make_async_copy(source, target, load_small.at[at])
        for at, (source, target) in enumerate(
            ((list_hbm, list_ref), (count_hbm, count_ref), (mask_hbm, mask_ref))
        )
    ]
    def tile_at(t):
        return pl.ds(t // tile_cols * TILE, TILE), pl.ds(t % tile_cols * TILE, TILE)

    amp_loads = [
        pltpu.make_async_copy(amp_hbm.at[tile_at(t)], amp.at[t], load_amp.at[t])
        for t in range(tiles)
    ]
    for load in small_loads:
        load.start()
    for load in amp_loads:
        load.start()
    for load in int_loads:
        load.start()

    barrier = pltpu.get_barrier_semaphore()
    partners = (
        (sibling, None), (across, None), (above, has_above), (below, has_below),
        (right, has_right), (left, has_left),
    )
    for partner, exists in partners:
        def greet(partner=partner):
            pl.semaphore_signal(barrier, inc=1, device_id=partner, device_id_type=MESH)
        if exists is None:
            greet()
        else:
            pl.when(exists)(greet)
    groups = [(0, 1), (1, live - 1)] if live > 1 else [(0, 1)]

    def amp_copy(source, slot, way, target):
        first, count = groups[slot]
        ref = packed.at[source, pl.ds(first, count)]
        return pltpu.make_async_remote_copy(
            src_ref=ref, dst_ref=ref,
            send_sem=amp_send.at[way, source, slot], recv_sem=amp_recv.at[source, slot],
            device_id=target, device_id_type=MESH,
        )

    def slot_copy(source, way, target):
        ref = slots.at[source]
        return pltpu.make_async_remote_copy(
            src_ref=ref, dst_ref=ref,
            send_sem=slot_send.at[way, source], recv_sem=slot_recv.at[source],
            device_id=target, device_id_type=MESH,
        )

    def int_copy(source, at, way, target, count=1):
        ref = ints.at[source, pl.ds(at * piece, count * piece)]
        return pltpu.make_async_remote_copy(
            src_ref=ref, dst_ref=ref,
            send_sem=int_send.at[way, source, at], recv_sem=int_recv.at[source, at],
            device_id=target, device_id_type=MESH,
        )

    def place_copy(source):
        return pltpu.make_async_copy(
            slots.at[source], place_ref.at[source], load_place.at[source]
        )

    out_ref[...] = jnp.zeros_like(out_ref)
    part_high[live] = jnp.zeros((TILE, TILE), BF16)
    part_low[live] = jnp.zeros((TILE, TILE), BF16)
    for load in small_loads:
        load.wait()
    numbers = [
        jnp.where(
            jnp.full((1, TILE), count_ref[0, 0], jnp.int32) > s,
            jnp.full((1, TILE), list_ref[0, 0, s], jnp.int32),
            -1,
        )
        for s in range(live)
    ]
    for t in range(tiles):
        place = jnp.full((1, TILE), live, jnp.int32)
        for s in range(live):
            place = jnp.where(numbers[s] == t, s, place)
        slots[col, pl.ds(t, 1), :] = place
    place_copy(col).start()
    for load in amp_loads:
        load.wait()
    for s in range(live):
        packed[col, s] = amp[list_ref[0, 0, s]]

    for at in range(2 * pieces):
        int_loads[at].wait()
        span = pl.ds(at * piece, piece)
        for c in range(int_cols // TILE):
            keep = mask_ref[c, at * piece // TILE].astype(F32)
            cols = pl.ds(c * TILE, TILE)
            ints[pair, span, cols] = ints[pair, span, cols] * keep

    peers = 2
    for _, exists in partners[2:]:
        peers += jnp.where(exists, 1, 0)
    pl.semaphore_wait(barrier, peers)

    def send_own_amp(copy):
        pl.when(has_above)(lambda: copy(0, above).start())
        pl.when(has_below)(lambda: copy(1, below).start())
        copy(2, sibling).start()

    def send_row(source, at, count=1):
        pl.when(has_right)(lambda: int_copy(source, at, 0, right, count).start())
        pl.when(has_left)(lambda: int_copy(source, at, 1, left, count).start())

    send_own_amp(lambda way, target: slot_copy(col, way, target))
    for s in range(max(len(groups), pieces)):
        if s < len(groups):
            send_own_amp(lambda way, target, s=s: amp_copy(col, s, way, target))
        if s < pieces:
            send_row(pair, s)
            int_copy(pair, pieces + s, 2, across).start()
    send_row(pair, pieces, pieces)
    int_copy(pair, 0, 2, across, pieces).start()

    def amp_slot(source):
        return jnp.abs(source // CORES - line_at)

    def int_slot(source, part):
        away = jnp.abs(source % wide - low_at)
        same = source // wide == high_at
        near = jnp.where(part == 0, away, jnp.where(away > 0, away + 1, 0))
        far = jnp.where(part == 0, away + 2, jnp.where(away > 0, away + 2, 1))
        return jnp.where(same, near, far)

    def step(now, _):
        def pass_amp(source, exists, way, target, more):
            @when(now >= 1, exists)
            def _():
                slot_copy(source, way, target).wait_recv()
                place_copy(source).start()
                pl.when(more)(lambda: slot_copy(source, way, target).start())
                slot_copy(source, 2, sibling).start()

        def pass_tile(source, s, exists, way, target, more):
            @when(now >= 1, exists)
            def _():
                amp_copy(source, s, way, target).wait_recv()
                pl.when(more)(lambda: amp_copy(source, s, way, target).start())
                amp_copy(source, s, 2, sibling).start()

        def pass_row(source, at, away, across_too, count=1):
            def one(side, exists, way, target, more):
                origin = source + side * away

                @when(away >= 1, exists)
                def _():
                    int_copy(origin, at, way, target, count).wait_recv()
                    pl.when(more)(lambda: int_copy(origin, at, way, target, count).start())
                    if across_too:
                        int_copy(origin, at, 2, across).start()

            one(-1, low_at - away >= 0, 0, right, has_right)
            one(1, low_at + away < wide, 1, left, has_left)

        lower, upper = col - CORES * now, col + CORES * now
        pass_amp(lower, line_at - now >= 0, 0, above, has_above)
        pass_amp(upper, line_at + now < line, 1, below, has_below)
        other = (1 - high_at) * wide + low_at
        for s in range(max(len(groups), pieces)):
            if s < len(groups):
                pass_tile(lower, s, line_at - now >= 0, 0, above, has_above)
                pass_tile(upper, s, line_at + now < line, 1, below, has_below)
            if s < pieces:
                pass_row(pair, s, now, True)

                @when(now == 1)
                def _(s=s):
                    int_copy(other, pieces + s, 2, across).wait_recv()
                    send_row(other, pieces + s)

        away = now - 2
        pass_row(pair, pieces, now - 1, False, pieces)
        pl.when(away == 0)(lambda: int_copy(other, 0, 2, across, pieces).wait_recv())
        for u in range(pieces):
            pass_row(other, pieces + u, away, False)
            for side, exists in ((-1, low_at - away >= 0), (1, low_at + away < wide)):
                @when(away >= 1, exists)
                def _(side=side, u=u):
                    int_copy(other + side * away, u, 2, across).wait_recv()

        def from_sibling(source):
            slot_copy(source, 2, sibling).wait_recv()
            place_copy(source).start()
            for s in range(len(groups)):
                amp_copy(source, s, 2, sibling).wait_recv()

        @pl.loop(0, n_pair * 2)
        def _(block):
            source, part = block // 2, block % 2

            @pl.when(int_slot(source, part) == now)
            def _():
                span = pl.ds(pl.multiple_of(part * half, half), half)
                value = ints[source, span]
                b_high[source, span], b_low[source, span] = split(value)

        mate = line_at * CORES + 1 - core

        @pl.loop(0, CORES)
        def _(turn):
            @pl.when(turn == 1)
            def _():
                pl.when(line_at - now >= 0)(lambda: from_sibling(mate - CORES * now))
                when(now >= 1, line_at + now < line)(lambda: from_sibling(mate + CORES * now))

            @pl.loop(0, line)
            def _(place_at):
                source = place_at * CORES + (core + turn) % CORES

                @pl.when(amp_slot(source) == now)
                def _():
                    for s in range(live):
                        part_high[s], part_low[s] = split(packed[source, s])
                    place_copy(source).wait()
                    for t in range(tiles):
                        place = place_ref[source, t, 0]
                        a_high[(source, *tile_at(t))] = part_high[place]
                        a_low[(source, *tile_at(t))] = part_low[place]

                start = source * depth
                origin, offset = start // int_rows, start % int_rows
                due = jnp.maximum(amp_slot(source), int_slot(origin, offset // half))

                @pl.when(due == now)
                def _():
                    span = pl.ds(pl.multiple_of(offset, depth), depth)
                    high, low = b_high[origin, span], b_low[origin, span]
                    first = a_high[source]
                    total = jnp.dot(first, high, preferred_element_type=F32)
                    total += jnp.dot(first, low, preferred_element_type=F32)
                    total += jnp.dot(a_low[source], high, preferred_element_type=F32)
                    out_ref[...] += total

        return 0

    steps = max(line - 1, wide + 1)
    lax.fori_loop(0, steps + 1, step, 0)

    @pl.loop(0, n_col)
    def _(source):
        mine = source % CORES == core
        at = source // CORES

        def drain(way, target):
            slot_copy(source, way, target).wait_send()
            for s in range(len(groups)):
                amp_copy(source, s, way, target).wait_send()

        when(mine, at <= line_at, has_above)(lambda: drain(0, above))
        when(mine, at >= line_at, has_below)(lambda: drain(1, below))
        pl.when(mine)(lambda: drain(2, sibling))

    @pl.loop(0, n_pair)
    def _(source):
        same = source // wide == high_at
        at = source % wide

        def drain(first, way, target, count=1):
            for u in range(0, pieces, count):
                int_copy(source, first + u, way, target, count).wait_send()

        to_right, to_left = (at <= low_at, has_right), (at >= low_at, has_left)
        when(same, *to_right)(lambda: drain(0, 0, right))
        when(same, *to_left)(lambda: drain(0, 1, left))
        when(same, at != low_at)(lambda: drain(0, 2, across))
        when(same, at == low_at)(lambda: drain(0, 2, across, pieces))
        when(same, *to_right)(lambda: drain(pieces, 0, right, pieces))
        when(same, *to_left)(lambda: drain(pieces, 1, left, pieces))
        when(~same, *to_right)(lambda: drain(pieces, 0, right))
        when(~same, *to_left)(lambda: drain(pieces, 1, left))
        pl.when(source == pair)(lambda: drain(pieces, 2, across))


def local(n_pair, n_col, amplitudes, integrals, amp_tiles, amp_count, int_mask):
    rows, depth = amplitudes.shape
    int_rows, int_cols = integrals.shape
    live = amp_tiles.shape[-1]
    tiles = (rows // TILE) * (depth // TILE)
    half = int_rows // 2
    assert n_pair % 2 == 0 and n_col % CORES == 0
    assert half % depth == 0 and half % TILE == 0
    pieces = int_rows // TILE
    scratch = [
        pltpu.SMEM(amp_tiles.shape, jnp.int32),
        pltpu.SMEM(amp_count.shape, jnp.int32),
        pltpu.SMEM(int_mask.shape[::-1], jnp.int32),
        pltpu.SMEM((n_col, tiles, TILE), jnp.int32),
        pltpu.VMEM((tiles, TILE, TILE), F32),
        pltpu.VMEM((live + 1, TILE, TILE), BF16),
        pltpu.VMEM((live + 1, TILE, TILE), BF16),
        pltpu.VMEM((n_col, live, TILE, TILE), F32),
        pltpu.VMEM((n_col, tiles, TILE), jnp.int32),
        pltpu.VMEM((n_pair, int_rows, int_cols), F32),
        pltpu.VMEM((n_col, rows, depth), BF16),
        pltpu.VMEM((n_col, rows, depth), BF16),
        pltpu.VMEM((n_pair, int_rows, int_cols), BF16),
        pltpu.VMEM((n_pair, int_rows, int_cols), BF16),
        pltpu.SemaphoreType.DMA((3,)),
        pltpu.SemaphoreType.DMA((tiles,)),
        pltpu.SemaphoreType.DMA((pieces,)),
        pltpu.SemaphoreType.DMA((n_col,)),
        pltpu.SemaphoreType.DMA((n_col, live)),
        pltpu.SemaphoreType.DMA((3, n_col, live)),
        pltpu.SemaphoreType.DMA((n_col,)),
        pltpu.SemaphoreType.DMA((3, n_col)),
        pltpu.SemaphoreType.DMA((n_pair, pieces)),
        pltpu.SemaphoreType.DMA((3, n_pair, pieces)),
    ]
    return pl.pallas_call(
        functools.partial(kernel, n_pair, n_col),
        out_shape=pltpu.VMEM((rows, int_cols), F32),
        in_specs=[pl.BlockSpec(memory_space=pltpu.HBM)] * 5,
        out_specs=pl.BlockSpec(memory_space=pltpu.VMEM),
        scratch_shapes=scratch,
        compiler_params=pltpu.CompilerParams(
            collective_id=0, has_side_effects=True, vmem_limit_bytes=VMEM_BYTES
        ),
        cost_estimate=pl.CostEstimate(
            flops=6 * rows * depth * n_col * int_cols,
            bytes_accessed=4 * rows * (2 * depth + int_cols),
            transcendentals=0,
        ),
        name="ladder",
    )(amp_tiles, amp_count, int_mask.T, amplitudes, integrals)


def solution(mesh):
    return jax.shard_map(
        functools.partial(local, mesh.shape["pair"], mesh.shape["col"]),
        mesh=mesh,
        in_specs=(
            P("pair", "col"),
            P("pair", "col"),
            P("pair", "col", None),
            P("pair", "col"),
            P("pair", "col"),
        ),
        out_specs=P("pair", "col"),
        check_vma=False,
    )
```

```python
import functools

import jax
import jax.numpy as jnp
from jax import lax
from jax.experimental import pallas as pl
from jax.experimental.pallas import tpu as pltpu
from jax.sharding import PartitionSpec as P

TILE = 128
CORES = 2
VMEM_BYTES = 60 << 20
MESH = pl.DeviceIdType.MESH
BF16 = jnp.bfloat16
F32 = jnp.float32


def split(value):
    high = value.astype(BF16)
    return high, (value - high.astype(F32)).astype(BF16)


def div(value, by):
    return lax.div(value, jnp.int32(by))


def rem(value, by):
    return lax.rem(value, jnp.int32(by))


def when(*conditions):
    together = conditions[0]
    for condition in conditions[1:]:
        together = jnp.logical_and(together, condition)
    return pl.when(together)


def kernel(
    n_pair, n_col, list_hbm, count_hbm, mask_hbm, amp_hbm, int_hbm, out_ref,
    list_ref, count_ref, mask_ref, place_ref, amp, part_high, part_low, packed, slots, ints, a_high, a_low, b_high, b_low,
    load_small, load_amp, load_int, load_place, amp_recv, amp_send, slot_recv, slot_send, int_recv, int_send,
):
    live = packed.shape[1]
    rows, depth = a_high.shape[1:]
    tile_cols = depth // TILE
    tiles = amp.shape[0]
    int_rows, int_cols = ints.shape[1:]
    half = int_rows // 2
    piece = TILE
    pieces = half // piece

    pair, col = lax.axis_index("pair"), lax.axis_index("col")
    line, line_at, core = n_col // CORES, col // CORES, col % CORES
    wide = n_pair // 2
    high_at, low_at = pair // wide, pair % wide

    sibling = {"col": line_at * CORES + 1 - core}
    above, below = {"col": col + CORES}, {"col": col - CORES}
    across = {"pair": (1 - high_at) * wide + low_at}
    right, left = {"pair": pair + 1}, {"pair": pair - 1}
    has_above, has_below = line_at < line - 1, line_at > 0
    has_right, has_left = low_at < wide - 1, low_at > 0

    int_loads = [
        pltpu.make_async_copy(
            int_hbm.at[pl.ds(at * piece, piece)],
            ints.at[pair, pl.ds(at * piece, piece)],
            load_int.at[at],
        )
        for at in range(2 * pieces)
    ]
    small_loads = [
        pltpu.make_async_copy(source, target, load_small.at[at])
        for at, (source, target) in enumerate(
            ((list_hbm, list_ref), (count_hbm, count_ref), (mask_hbm, mask_ref))
        )
    ]
    def tile_at(t):
        return pl.ds(t // tile_cols * TILE, TILE), pl.ds(t % tile_cols * TILE, TILE)

    amp_loads = [
        pltpu.make_async_copy(amp_hbm.at[tile_at(t)], amp.at[t], load_amp.at[t])
        for t in range(tiles)
    ]
    for load in small_loads:
        load.start()
    for load in amp_loads:
        load.start()
    for load in int_loads:
        load.start()

    barrier = pltpu.get_barrier_semaphore()
    partners = (
        (sibling, None), (across, None), (above, has_above), (below, has_below),
        (right, has_right), (left, has_left),
    )
    for partner, exists in partners:
        def greet(partner=partner):
            pl.semaphore_signal(barrier, inc=1, device_id=partner, device_id_type=MESH)
        if exists is None:
            greet()
        else:
            pl.when(exists)(greet)
    groups = [(0, 1), (1, live - 1)] if live > 1 else [(0, 1)]

    def amp_copy(source, slot, way, target):
        first, count = groups[slot]
        ref = packed.at[source, pl.ds(first, count)]
        return pltpu.make_async_remote_copy(
            src_ref=ref, dst_ref=ref,
            send_sem=amp_send.at[way, source, slot], recv_sem=amp_recv.at[source, slot],
            device_id=target, device_id_type=MESH,
        )

    def slot_copy(source, way, target):
        ref = slots.at[source]
        return pltpu.make_async_remote_copy(
            src_ref=ref, dst_ref=ref,
            send_sem=slot_send.at[way, source], recv_sem=slot_recv.at[source],
            device_id=target, device_id_type=MESH,
        )

    def int_copy(source, at, way, target, count=1):
        ref = ints.at[source, pl.ds(at * piece, count * piece)]
        return pltpu.make_async_remote_copy(
            src_ref=ref, dst_ref=ref,
            send_sem=int_send.at[way, source, at], recv_sem=int_recv.at[source, at],
            device_id=target, device_id_type=MESH,
        )

    def place_copy(source):
        return pltpu.make_async_copy(
            slots.at[source], place_ref.at[source], load_place.at[source]
        )

    part_high[live] = jnp.zeros((TILE, TILE), BF16)
    part_low[live] = jnp.zeros((TILE, TILE), BF16)
    for load in small_loads:
        load.wait()
    numbers = [
        jnp.where(
            jnp.full((1, TILE), count_ref[0, 0], jnp.int32) > s,
            jnp.full((1, TILE), list_ref[0, 0, s], jnp.int32),
            -1,
        )
        for s in range(live)
    ]
    for t in range(tiles):
        place = jnp.full((1, TILE), live, jnp.int32)
        for s in range(live):
            place = jnp.where(numbers[s] == t, s, place)
        slots[col, pl.ds(t, 1), :] = place
    place_copy(col).start()
    for load in amp_loads:
        load.wait()
    for s in range(live):
        packed[col, s] = amp[list_ref[0, 0, s]]

    for at in range(2 * pieces):
        int_loads[at].wait()
        span = pl.ds(at * piece, piece)
        for c in range(int_cols // TILE):
            keep = mask_ref[c, at * piece // TILE].astype(F32)
            cols = pl.ds(c * TILE, TILE)
            ints[pair, span, cols] = ints[pair, span, cols] * keep

    peers = 2
    for _, exists in partners[2:]:
        peers += jnp.where(exists, 1, 0)
    pl.semaphore_wait(barrier, peers)

    def send_own_amp(copy):
        pl.when(has_above)(lambda: copy(0, above).start())
        pl.when(has_below)(lambda: copy(1, below).start())
        copy(2, sibling).start()

    def send_row(source, at, count=1):
        pl.when(has_right)(lambda: int_copy(source, at, 0, right, count).start())
        pl.when(has_left)(lambda: int_copy(source, at, 1, left, count).start())

    send_own_amp(lambda way, target: slot_copy(col, way, target))
    for s in range(max(len(groups), pieces)):
        if s < len(groups):
            send_own_amp(lambda way, target, s=s: amp_copy(col, s, way, target))
        if s < pieces:
            send_row(pair, s)
            int_copy(pair, pieces + s, 2, across).start()
    send_row(pair, pieces, pieces)
    int_copy(pair, 0, 2, across, pieces).start()

    out_ref[...] = jnp.zeros_like(out_ref)

    def amp_slot(source):
        return jnp.abs(div(source, CORES) - line_at)

    def int_slot(source, part):
        away = jnp.abs(rem(source, wide) - low_at)
        same = div(source, wide) == high_at
        near = jnp.where(part == 0, away, jnp.where(away > 0, away + 1, 0))
        far = jnp.where(part == 0, away + 2, jnp.where(away > 0, away + 2, 1))
        return jnp.where(same, near, far)

    steps = max(line - 1, wide + 1)

    def drain_amp(source, way, target):
        slot_copy(source, way, target).wait_send()
        for s in range(len(groups)):
            amp_copy(source, s, way, target).wait_send()

    def drain_early():
        @pl.loop(0, n_col)
        def _(source):
            mine = rem(source, CORES) == core
            at = div(source, CORES)

            when(mine, at <= line_at, has_above)(lambda: drain_amp(source, 0, above))
            when(mine, at >= line_at, has_below)(lambda: drain_amp(source, 1, below))
            when(mine, jnp.abs(at - line_at) < steps)(lambda: drain_amp(source, 2, sibling))

        @pl.loop(0, n_pair)
        def _(source):
            same = div(source, wide) == high_at
            at = rem(source, wide)

            def drain(first, way, target, count=1):
                for u in range(0, pieces, count):
                    int_copy(source, first + u, way, target, count).wait_send()

            to_right, to_left = (at <= low_at, has_right), (at >= low_at, has_left)
            when(same, *to_right)(lambda: drain(0, 0, right))
            when(same, *to_left)(lambda: drain(0, 1, left))
            when(same, at != low_at)(lambda: drain(0, 2, across))
            when(same, at == low_at)(lambda: drain(0, 2, across, pieces))
            when(same, *to_right)(lambda: drain(pieces, 0, right, pieces))
            when(same, *to_left)(lambda: drain(pieces, 1, left, pieces))
            when(~same, *to_right)(lambda: drain(pieces, 0, right))
            when(~same, *to_left)(lambda: drain(pieces, 1, left))
            pl.when(source == pair)(lambda: drain(pieces, 2, across))

    def step(now, _):
        pl.when(now == steps)(drain_early)

        def pass_amp(source, exists, way, target, more):
            @when(now >= 1, exists)
            def _():
                slot_copy(source, way, target).wait_recv()
                place_copy(source).start()
                pl.when(more)(lambda: slot_copy(source, way, target).start())
                slot_copy(source, 2, sibling).start()

        def pass_tile(source, s, exists, way, target, more):
            @when(now >= 1, exists)
            def _():
                amp_copy(source, s, way, target).wait_recv()
                pl.when(more)(lambda: amp_copy(source, s, way, target).start())
                amp_copy(source, s, 2, sibling).start()

        def pass_row(source, at, away, across_too, count=1):
            def one(side, exists, way, target, more):
                origin = source + side * away

                @when(away >= 1, exists)
                def _():
                    int_copy(origin, at, way, target, count).wait_recv()
                    pl.when(more)(lambda: int_copy(origin, at, way, target, count).start())
                    if across_too:
                        int_copy(origin, at, 2, across).start()

            one(-1, low_at - away >= 0, 0, right, has_right)
            one(1, low_at + away < wide, 1, left, has_left)

        lower, upper = col - CORES * now, col + CORES * now
        pass_amp(lower, line_at - now >= 0, 0, above, has_above)
        pass_amp(upper, line_at + now < line, 1, below, has_below)
        other = (1 - high_at) * wide + low_at
        for s in range(max(len(groups), pieces)):
            if s < len(groups):
                pass_tile(lower, s, line_at - now >= 0, 0, above, has_above)
                pass_tile(upper, s, line_at + now < line, 1, below, has_below)
            if s < pieces:
                pass_row(pair, s, now, True)

                @when(now == 1)
                def _(s=s):
                    int_copy(other, pieces + s, 2, across).wait_recv()
                    send_row(other, pieces + s)

        away = now - 2
        pass_row(pair, pieces, now - 1, False, pieces)
        pl.when(away == 0)(lambda: int_copy(other, 0, 2, across, pieces).wait_recv())
        for u in range(pieces):
            pass_row(other, pieces + u, away, False)
            for side, exists in ((-1, low_at - away >= 0), (1, low_at + away < wide)):
                @when(away >= 1, exists)
                def _(side=side, u=u):
                    int_copy(other + side * away, u, 2, across).wait_recv()

        def from_sibling(source):
            slot_copy(source, 2, sibling).wait_recv()
            place_copy(source).start()
            for s in range(len(groups)):
                amp_copy(source, s, 2, sibling).wait_recv()

        @pl.loop(0, n_pair * 2)
        def _(block):
            source, part = div(block, 2), rem(block, 2)

            @pl.when(int_slot(source, part) == now)
            def _():
                span = pl.ds(pl.multiple_of(part * half, half), half)
                value = ints[source, span]
                b_high[source, span], b_low[source, span] = split(value)

        mate = line_at * CORES + 1 - core

        @pl.loop(0, CORES)
        def _(turn):
            @pl.when(turn == 1)
            def _():
                pl.when(line_at - now >= 0)(lambda: from_sibling(mate - CORES * now))
                when(now >= 1, line_at + now < line)(lambda: from_sibling(mate + CORES * now))

            other_core = rem(core + turn, CORES)

            @pl.loop(0, 2)
            def _(side):
                place_at = line_at + (2 * side - 1) * now
                source = place_at * CORES + other_core

                @when(place_at >= 0, place_at < line, (side == 0) | (now > 0))
                def _():
                    for s in range(live):
                        part_high[s], part_low[s] = split(packed[source, s])
                    place_copy(source).wait()
                    for t in range(tiles):
                        place = place_ref[source, t, 0]
                        a_high[(source, *tile_at(t))] = part_high[place]
                        a_low[(source, *tile_at(t))] = part_low[place]

            @pl.loop(0, line)
            def _(place_at):
                source = place_at * CORES + other_core
                start = source * depth
                origin, offset = div(start, int_rows), rem(start, int_rows)
                due = jnp.maximum(amp_slot(source), int_slot(origin, div(offset, half)))

                @pl.when(due == now)
                def _():
                    span = pl.ds(pl.multiple_of(offset, depth), depth)
                    high, low = b_high[origin, span], b_low[origin, span]
                    first = a_high[source]
                    total = jnp.dot(first, high, preferred_element_type=F32)
                    total += jnp.dot(first, low, preferred_element_type=F32)
                    total += jnp.dot(a_low[source], high, preferred_element_type=F32)
                    out_ref[...] += total

        return 0

    lax.fori_loop(0, steps + 1, step, 0)

    for side in (-1, 1):
        ending = line_at + side * steps

        @when(ending >= 0, ending < line)
        def _(ending=ending):
            drain_amp(ending * CORES + core, 2, sibling)


def local(n_pair, n_col, amplitudes, integrals, amp_tiles, amp_count, int_mask):
    rows, depth = amplitudes.shape
    int_rows, int_cols = integrals.shape
    live = amp_tiles.shape[-1]
    tiles = (rows // TILE) * (depth // TILE)
    half = int_rows // 2
    assert n_pair % 2 == 0 and n_col % CORES == 0
    assert half % depth == 0 and half % TILE == 0
    pieces = int_rows // TILE
    scratch = [
        pltpu.SMEM(amp_tiles.shape, jnp.int32),
        pltpu.SMEM(amp_count.shape, jnp.int32),
        pltpu.SMEM(int_mask.shape[::-1], jnp.int32),
        pltpu.SMEM((n_col, tiles, TILE), jnp.int32),
        pltpu.VMEM((tiles, TILE, TILE), F32),
        pltpu.VMEM((live + 1, TILE, TILE), BF16),
        pltpu.VMEM((live + 1, TILE, TILE), BF16),
        pltpu.VMEM((n_col, live, TILE, TILE), F32),
        pltpu.VMEM((n_col, tiles, TILE), jnp.int32),
        pltpu.VMEM((n_pair, int_rows, int_cols), F32),
        pltpu.VMEM((n_col, rows, depth), BF16),
        pltpu.VMEM((n_col, rows, depth), BF16),
        pltpu.VMEM((n_pair, int_rows, int_cols), BF16),
        pltpu.VMEM((n_pair, int_rows, int_cols), BF16),
        pltpu.SemaphoreType.DMA((3,)),
        pltpu.SemaphoreType.DMA((tiles,)),
        pltpu.SemaphoreType.DMA((pieces,)),
        pltpu.SemaphoreType.DMA((n_col,)),
        pltpu.SemaphoreType.DMA((n_col, live)),
        pltpu.SemaphoreType.DMA((3, n_col, live)),
        pltpu.SemaphoreType.DMA((n_col,)),
        pltpu.SemaphoreType.DMA((3, n_col)),
        pltpu.SemaphoreType.DMA((n_pair, pieces)),
        pltpu.SemaphoreType.DMA((3, n_pair, pieces)),
    ]
    return pl.pallas_call(
        functools.partial(kernel, n_pair, n_col),
        out_shape=pltpu.VMEM((rows, int_cols), F32),
        in_specs=[pl.BlockSpec(memory_space=pltpu.HBM)] * 5,
        out_specs=pl.BlockSpec(memory_space=pltpu.VMEM),
        scratch_shapes=scratch,
        compiler_params=pltpu.CompilerParams(
            collective_id=0, has_side_effects=True, vmem_limit_bytes=VMEM_BYTES
        ),
        cost_estimate=pl.CostEstimate(
            flops=6 * rows * depth * n_col * int_cols,
            bytes_accessed=4 * rows * (2 * depth + int_cols),
            transcendentals=0,
        ),
        name="ladder",
    )(amp_tiles, amp_count, int_mask.T, amplitudes, integrals)


def solution(mesh):
    return jax.shard_map(
        functools.partial(local, mesh.shape["pair"], mesh.shape["col"]),
        mesh=mesh,
        in_specs=(
            P("pair", "col"),
            P("pair", "col"),
            P("pair", "col", None),
            P("pair", "col"),
            P("pair", "col"),
        ),
        out_specs=P("pair", "col"),
        check_vma=False,
    )
```

```python
import functools

import jax
import jax.numpy as jnp
from jax import lax
from jax.experimental import pallas as pl
from jax.experimental.pallas import tpu as pltpu
from jax.sharding import PartitionSpec as P

TILE = 128
CORES = 2
VMEM_BYTES = 60 << 20
MESH = pl.DeviceIdType.MESH
BF16 = jnp.bfloat16
F32 = jnp.float32


def split(value):
    high = value.astype(BF16)
    return high, (value - high.astype(F32)).astype(BF16)


def div(value, by):
    return lax.div(value, jnp.int32(by))


def rem(value, by):
    return lax.rem(value, jnp.int32(by))


def when(*conditions):
    together = conditions[0]
    for condition in conditions[1:]:
        together = jnp.logical_and(together, condition)
    return pl.when(together)


def kernel(
    n_pair, n_col, list_hbm, count_hbm, mask_hbm, amp_hbm, int_hbm, out_ref,
    list_ref, count_ref, mask_ref, place_ref, amp, part_high, part_low, packed, slots, ints, a_high, a_low, b_high, b_low,
    load_small, load_amp, load_int, load_place, amp_recv, amp_send, slot_recv, slot_send, int_recv, int_send,
):
    live = packed.shape[1]
    rows, depth = a_high.shape[1:]
    tile_cols = depth // TILE
    tiles = amp.shape[0]
    int_rows, int_cols = ints.shape[1:]
    half = int_rows // 2
    piece = TILE
    pieces = half // piece

    pair, col = lax.axis_index("pair"), lax.axis_index("col")
    line, line_at, core = n_col // CORES, col // CORES, col % CORES
    wide = n_pair // 2
    high_at, low_at = pair // wide, pair % wide

    sibling = {"col": line_at * CORES + 1 - core}
    above, below = {"col": col + CORES}, {"col": col - CORES}
    across = {"pair": (1 - high_at) * wide + low_at}
    right, left = {"pair": pair + 1}, {"pair": pair - 1}
    has_above, has_below = line_at < line - 1, line_at > 0
    has_right, has_left = low_at < wide - 1, low_at > 0

    int_loads = [
        pltpu.make_async_copy(
            int_hbm.at[pl.ds(at * piece, piece)],
            ints.at[pair, pl.ds(at * piece, piece)],
            load_int.at[at],
        )
        for at in range(2 * pieces)
    ]
    small_loads = [
        pltpu.make_async_copy(source, target, load_small.at[at])
        for at, (source, target) in enumerate(
            ((list_hbm, list_ref), (count_hbm, count_ref), (mask_hbm, mask_ref))
        )
    ]
    def tile_at(t):
        return pl.ds(t // tile_cols * TILE, TILE), pl.ds(t % tile_cols * TILE, TILE)

    amp_loads = [
        pltpu.make_async_copy(amp_hbm.at[tile_at(t)], amp.at[t], load_amp.at[t])
        for t in range(tiles)
    ]
    for load in small_loads:
        load.start()
    for load in amp_loads:
        load.start()
    for load in int_loads:
        load.start()

    barrier = pltpu.get_barrier_semaphore()
    partners = (
        (sibling, None), (across, None), (above, has_above), (below, has_below),
        (right, has_right), (left, has_left),
    )
    for partner, exists in partners:
        def greet(partner=partner):
            pl.semaphore_signal(barrier, inc=1, device_id=partner, device_id_type=MESH)
        if exists is None:
            greet()
        else:
            pl.when(exists)(greet)
    groups = [(0, 1), (1, live - 1)] if live > 1 else [(0, 1)]

    def amp_copy(source, slot, way, target):
        first, count = groups[slot]
        ref = packed.at[source, pl.ds(first, count)]
        return pltpu.make_async_remote_copy(
            src_ref=ref, dst_ref=ref,
            send_sem=amp_send.at[way, source, slot], recv_sem=amp_recv.at[source, slot],
            device_id=target, device_id_type=MESH,
        )

    def slot_copy(source, way, target):
        ref = slots.at[source]
        return pltpu.make_async_remote_copy(
            src_ref=ref, dst_ref=ref,
            send_sem=slot_send.at[way, source], recv_sem=slot_recv.at[source],
            device_id=target, device_id_type=MESH,
        )

    def int_copy(source, at, way, target, count=1):
        ref = ints.at[source, pl.ds(at * piece, count * piece)]
        return pltpu.make_async_remote_copy(
            src_ref=ref, dst_ref=ref,
            send_sem=int_send.at[way, source, at], recv_sem=int_recv.at[source, at],
            device_id=target, device_id_type=MESH,
        )

    def place_copy(source):
        return pltpu.make_async_copy(
            slots.at[source], place_ref.at[source], load_place.at[source]
        )

    part_high[live] = jnp.zeros((TILE, TILE), BF16)
    part_low[live] = jnp.zeros((TILE, TILE), BF16)
    for load in small_loads:
        load.wait()
    numbers = [
        jnp.where(
            jnp.full((1, TILE), count_ref[0, 0], jnp.int32) > s,
            jnp.full((1, TILE), list_ref[0, 0, s], jnp.int32),
            -1,
        )
        for s in range(live)
    ]
    for t in range(tiles):
        place = jnp.full((1, TILE), live, jnp.int32)
        for s in range(live):
            place = jnp.where(numbers[s] == t, s, place)
        slots[col, pl.ds(t, 1), :] = place
    place_copy(col).start()
    for load in amp_loads:
        load.wait()
    for s in range(live):
        packed[col, s] = amp[list_ref[0, 0, s]]

    for at in range(2 * pieces):
        int_loads[at].wait()
        span = pl.ds(at * piece, piece)
        for c in range(int_cols // TILE):
            keep = mask_ref[c, at * piece // TILE].astype(F32)
            cols = pl.ds(c * TILE, TILE)
            ints[pair, span, cols] = ints[pair, span, cols] * keep

    peers = 2
    for _, exists in partners[2:]:
        peers += jnp.where(exists, 1, 0)
    pl.semaphore_wait(barrier, peers)

    def send_own_amp(copy):
        pl.when(has_above)(lambda: copy(0, above).start())
        pl.when(has_below)(lambda: copy(1, below).start())
        copy(2, sibling).start()

    def send_row(source, at, count=1):
        pl.when(has_right)(lambda: int_copy(source, at, 0, right, count).start())
        pl.when(has_left)(lambda: int_copy(source, at, 1, left, count).start())

    send_own_amp(lambda way, target: slot_copy(col, way, target))
    for s in range(max(len(groups), pieces)):
        if s < len(groups):
            send_own_amp(lambda way, target, s=s: amp_copy(col, s, way, target))
        if s < pieces:
            send_row(pair, s)
            int_copy(pair, pieces + s, 2, across).start()
    send_row(pair, pieces, pieces)
    int_copy(pair, 0, 2, across, pieces).start()

    out_ref[...] = jnp.zeros_like(out_ref)

    def amp_slot(source):
        return jnp.abs(div(source, CORES) - line_at)

    def int_slot(source, part):
        away = jnp.abs(rem(source, wide) - low_at)
        same = div(source, wide) == high_at
        near = jnp.where(part == 0, away, jnp.where(away > 0, away + 1, 0))
        far = jnp.where(part == 0, away + 2, jnp.where(away > 0, away + 2, 1))
        return jnp.where(same, near, far)

    steps = max(line - 1, wide + 1)

    def drain_amp(source, way, target):
        slot_copy(source, way, target).wait_send()
        for s in range(len(groups)):
            amp_copy(source, s, way, target).wait_send()

    def drain_early():
        @pl.loop(0, n_col)
        def _(source):
            mine = rem(source, CORES) == core
            at = div(source, CORES)

            when(mine, at <= line_at, has_above)(lambda: drain_amp(source, 0, above))
            when(mine, at >= line_at, has_below)(lambda: drain_amp(source, 1, below))
            when(mine, jnp.abs(at - line_at) < steps)(lambda: drain_amp(source, 2, sibling))

        @pl.loop(0, n_pair)
        def _(source):
            same = div(source, wide) == high_at
            at = rem(source, wide)

            def drain(first, way, target, count=1):
                for u in range(0, pieces, count):
                    int_copy(source, first + u, way, target, count).wait_send()

            to_right, to_left = (at <= low_at, has_right), (at >= low_at, has_left)
            when(same, *to_right)(lambda: drain(0, 0, right))
            when(same, *to_left)(lambda: drain(0, 1, left))
            when(same, at != low_at)(lambda: drain(0, 2, across))
            when(same, at == low_at)(lambda: drain(0, 2, across, pieces))
            when(same, *to_right)(lambda: drain(pieces, 0, right, pieces))
            when(same, *to_left)(lambda: drain(pieces, 1, left, pieces))
            when(~same, *to_right)(lambda: drain(pieces, 0, right))
            when(~same, *to_left)(lambda: drain(pieces, 1, left))
            pl.when(source == pair)(lambda: drain(pieces, 2, across))

    def step(now, _):
        pl.when(now == steps)(drain_early)

        def pass_amp(source, exists, way, target, more):
            @when(now >= 1, exists)
            def _():
                slot_copy(source, way, target).wait_recv()
                place_copy(source).start()
                pl.when(more)(lambda: slot_copy(source, way, target).start())
                slot_copy(source, 2, sibling).start()

        def pass_tile(source, s, exists, way, target, more):
            @when(now >= 1, exists)
            def _():
                amp_copy(source, s, way, target).wait_recv()
                pl.when(more)(lambda: amp_copy(source, s, way, target).start())
                amp_copy(source, s, 2, sibling).start()

        def pass_row(source, at, away, across_too, count=1):
            def one(side, exists, way, target, more):
                origin = source + side * away

                @when(away >= 1, exists)
                def _():
                    int_copy(origin, at, way, target, count).wait_recv()
                    pl.when(more)(lambda: int_copy(origin, at, way, target, count).start())
                    if across_too:
                        int_copy(origin, at, 2, across).start()

            one(-1, low_at - away >= 0, 0, right, has_right)
            one(1, low_at + away < wide, 1, left, has_left)

        lower, upper = col - CORES * now, col + CORES * now
        pass_amp(lower, line_at - now >= 0, 0, above, has_above)
        pass_amp(upper, line_at + now < line, 1, below, has_below)
        other = (1 - high_at) * wide + low_at
        for s in range(max(len(groups), pieces)):
            if s < len(groups):
                pass_tile(lower, s, line_at - now >= 0, 0, above, has_above)
                pass_tile(upper, s, line_at + now < line, 1, below, has_below)
            if s < pieces:
                pass_row(pair, s, now, True)

                @when(now == 1)
                def _(s=s):
                    int_copy(other, pieces + s, 2, across).wait_recv()
                    send_row(other, pieces + s)

        away = now - 2
        pass_row(pair, pieces, now - 1, False, pieces)
        pl.when(away == 0)(lambda: int_copy(other, 0, 2, across, pieces).wait_recv())
        for u in range(pieces):
            pass_row(other, pieces + u, away, False)
            for side, exists in ((-1, low_at - away >= 0), (1, low_at + away < wide)):
                @when(away >= 1, exists)
                def _(side=side, u=u):
                    int_copy(other + side * away, u, 2, across).wait_recv()

        def from_sibling(source):
            slot_copy(source, 2, sibling).wait_recv()
            place_copy(source).start()
            for s in range(len(groups)):
                amp_copy(source, s, 2, sibling).wait_recv()

        @pl.loop(0, n_pair * 2)
        def _(block):
            source, part = div(block, 2), rem(block, 2)

            @pl.when(int_slot(source, part) == now)
            def _():
                span = pl.ds(pl.multiple_of(part * half, half), half)
                value = ints[source, span]
                b_high[source, span], b_low[source, span] = split(value)

        mate = line_at * CORES + 1 - core

        @pl.loop(0, CORES)
        def _(turn):
            @pl.when(turn == 1)
            def _():
                pl.when(line_at - now >= 0)(lambda: from_sibling(mate - CORES * now))
                when(now >= 1, line_at + now < line)(lambda: from_sibling(mate + CORES * now))

            other_core = rem(core + turn, CORES)

            @pl.loop(0, 2)
            def _(side):
                place_at = line_at + (2 * side - 1) * now
                source = place_at * CORES + other_core

                @when(place_at >= 0, place_at < line, (side == 0) | (now > 0))
                def _():
                    for s in range(live):
                        part_high[s], part_low[s] = split(packed[source, s])
                    place_copy(source).wait()
                    for t in range(tiles):
                        place = place_ref[source, t, 0]
                        a_high[(source, *tile_at(t))] = part_high[place]
                        a_low[(source, *tile_at(t))] = part_low[place]

            @pl.loop(0, line)
            def _(place_at):
                source = place_at * CORES + other_core
                start = source * depth
                origin, offset = div(start, int_rows), rem(start, int_rows)
                due = jnp.maximum(amp_slot(source), int_slot(origin, div(offset, half)))

                @pl.when(due == now)
                def _():
                    span = pl.ds(pl.multiple_of(offset, depth), depth)
                    high, low = b_high[origin, span], b_low[origin, span]
                    first = a_high[source]
                    out_ref[...] += jnp.dot(
                        jnp.concatenate([first, a_low[source], first], axis=1),
                        jnp.concatenate([high, high, low], axis=0),
                        preferred_element_type=F32,
                    )

        return 0

    lax.fori_loop(0, steps + 1, step, 0)

    for side in (-1, 1):
        ending = line_at + side * steps

        @when(ending >= 0, ending < line)
        def _(ending=ending):
            drain_amp(ending * CORES + core, 2, sibling)


def local(n_pair, n_col, amplitudes, integrals, amp_tiles, amp_count, int_mask):
    rows, depth = amplitudes.shape
    int_rows, int_cols = integrals.shape
    live = amp_tiles.shape[-1]
    tiles = (rows // TILE) * (depth // TILE)
    half = int_rows // 2
    assert n_pair % 2 == 0 and n_col % CORES == 0
    assert half % depth == 0 and half % TILE == 0
    pieces = int_rows // TILE
    scratch = [
        pltpu.SMEM(amp_tiles.shape, jnp.int32),
        pltpu.SMEM(amp_count.shape, jnp.int32),
        pltpu.SMEM(int_mask.shape[::-1], jnp.int32),
        pltpu.SMEM((n_col, tiles, TILE), jnp.int32),
        pltpu.VMEM((tiles, TILE, TILE), F32),
        pltpu.VMEM((live + 1, TILE, TILE), BF16),
        pltpu.VMEM((live + 1, TILE, TILE), BF16),
        pltpu.VMEM((n_col, live, TILE, TILE), F32),
        pltpu.VMEM((n_col, tiles, TILE), jnp.int32),
        pltpu.VMEM((n_pair, int_rows, int_cols), F32),
        pltpu.VMEM((n_col, rows, depth), BF16),
        pltpu.VMEM((n_col, rows, depth), BF16),
        pltpu.VMEM((n_pair, int_rows, int_cols), BF16),
        pltpu.VMEM((n_pair, int_rows, int_cols), BF16),
        pltpu.SemaphoreType.DMA((3,)),
        pltpu.SemaphoreType.DMA((tiles,)),
        pltpu.SemaphoreType.DMA((pieces,)),
        pltpu.SemaphoreType.DMA((n_col,)),
        pltpu.SemaphoreType.DMA((n_col, live)),
        pltpu.SemaphoreType.DMA((3, n_col, live)),
        pltpu.SemaphoreType.DMA((n_col,)),
        pltpu.SemaphoreType.DMA((3, n_col)),
        pltpu.SemaphoreType.DMA((n_pair, pieces)),
        pltpu.SemaphoreType.DMA((3, n_pair, pieces)),
    ]
    return pl.pallas_call(
        functools.partial(kernel, n_pair, n_col),
        out_shape=pltpu.VMEM((rows, int_cols), F32),
        in_specs=[pl.BlockSpec(memory_space=pltpu.HBM)] * 5,
        out_specs=pl.BlockSpec(memory_space=pltpu.VMEM),
        scratch_shapes=scratch,
        compiler_params=pltpu.CompilerParams(
            collective_id=0, has_side_effects=True, vmem_limit_bytes=VMEM_BYTES
        ),
        cost_estimate=pl.CostEstimate(
            flops=6 * rows * depth * n_col * int_cols,
            bytes_accessed=4 * rows * (2 * depth + int_cols),
            transcendentals=0,
        ),
        name="ladder",
    )(amp_tiles, amp_count, int_mask.T, amplitudes, integrals)


def solution(mesh):
    return jax.shard_map(
        functools.partial(local, mesh.shape["pair"], mesh.shape["col"]),
        mesh=mesh,
        in_specs=(
            P("pair", "col"),
            P("pair", "col"),
            P("pair", "col", None),
            P("pair", "col"),
            P("pair", "col"),
        ),
        out_specs=P("pair", "col"),
        check_vma=False,
    )
```

```python
import functools

import jax
import jax.numpy as jnp
from jax import lax
from jax.experimental import pallas as pl
from jax.experimental.pallas import tpu as pltpu
from jax.sharding import PartitionSpec as P

TILE = 128
CORES = 2
VMEM_BYTES = 60 << 20
MESH = pl.DeviceIdType.MESH
BF16 = jnp.bfloat16
F32 = jnp.float32


def split(value):
    high = value.astype(BF16)
    return high, (value - high.astype(F32)).astype(BF16)


def div(value, by):
    return lax.div(value, jnp.int32(by))


def rem(value, by):
    return lax.rem(value, jnp.int32(by))


def when(*conditions):
    together = conditions[0]
    for condition in conditions[1:]:
        together = jnp.logical_and(together, condition)
    return pl.when(together)


def kernel(
    n_pair, n_col, list_hbm, count_hbm, mask_hbm, amp_hbm, int_hbm, out_ref,
    list_ref, count_ref, mask_ref, place_ref, amp, part_high, part_low, packed, slots, ints, a_high, a_low, b_high, b_low,
    load_small, load_amp, load_int, load_place, amp_recv, amp_send, slot_recv, slot_send, int_recv, int_send,
):
    live = packed.shape[1]
    rows, depth = a_high.shape[1:]
    tile_cols = depth // TILE
    tiles = amp.shape[0]
    int_rows, int_cols = ints.shape[1:]
    half = int_rows // 2
    piece = TILE
    pieces = half // piece

    pair, col = lax.axis_index("pair"), lax.axis_index("col")
    line, line_at, core = n_col // CORES, col // CORES, col % CORES
    wide = n_pair // 2
    high_at, low_at = pair // wide, pair % wide

    sibling = {"col": line_at * CORES + 1 - core}
    above, below = {"col": col + CORES}, {"col": col - CORES}
    across = {"pair": (1 - high_at) * wide + low_at}
    right, left = {"pair": pair + 1}, {"pair": pair - 1}
    has_above, has_below = line_at < line - 1, line_at > 0
    has_right, has_left = low_at < wide - 1, low_at > 0

    int_loads = [
        pltpu.make_async_copy(
            int_hbm.at[pl.ds(at * piece, piece)],
            ints.at[pair, pl.ds(at * piece, piece)],
            load_int.at[at],
        )
        for at in range(2 * pieces)
    ]
    small_loads = [
        pltpu.make_async_copy(source, target, load_small.at[at])
        for at, (source, target) in enumerate(
            ((list_hbm, list_ref), (count_hbm, count_ref), (mask_hbm, mask_ref))
        )
    ]
    def tile_at(t):
        return pl.ds(t // tile_cols * TILE, TILE), pl.ds(t % tile_cols * TILE, TILE)

    amp_loads = [
        pltpu.make_async_copy(amp_hbm.at[tile_at(t)], amp.at[t], load_amp.at[t])
        for t in range(tiles)
    ]
    for load in small_loads:
        load.start()
    for load in amp_loads:
        load.start()
    for load in int_loads:
        load.start()

    barrier = pltpu.get_barrier_semaphore()
    partners = (
        (sibling, None), (across, None), (above, has_above), (below, has_below),
        (right, has_right), (left, has_left),
    )
    for partner, exists in partners:
        def greet(partner=partner):
            pl.semaphore_signal(barrier, inc=1, device_id=partner, device_id_type=MESH)
        if exists is None:
            greet()
        else:
            pl.when(exists)(greet)
    groups = [(0, 1), (1, live - 1)] if live > 1 else [(0, 1)]

    def amp_copy(source, slot, way, target):
        first, count = groups[slot]
        ref = packed.at[source, pl.ds(first, count)]
        return pltpu.make_async_remote_copy(
            src_ref=ref, dst_ref=ref,
            send_sem=amp_send.at[way, source, slot], recv_sem=amp_recv.at[source, slot],
            device_id=target, device_id_type=MESH,
        )

    def slot_copy(source, way, target):
        ref = slots.at[source]
        return pltpu.make_async_remote_copy(
            src_ref=ref, dst_ref=ref,
            send_sem=slot_send.at[way, source], recv_sem=slot_recv.at[source],
            device_id=target, device_id_type=MESH,
        )

    def int_copy(source, at, way, target, count=1):
        ref = ints.at[source, pl.ds(at * piece, count * piece)]
        return pltpu.make_async_remote_copy(
            src_ref=ref, dst_ref=ref,
            send_sem=int_send.at[way, source, at], recv_sem=int_recv.at[source, at],
            device_id=target, device_id_type=MESH,
        )

    def place_copy(source):
        return pltpu.make_async_copy(
            slots.at[source], place_ref.at[source], load_place.at[source]
        )

    part_high[live] = jnp.zeros((TILE, TILE), BF16)
    part_low[live] = jnp.zeros((TILE, TILE), BF16)
    for load in small_loads:
        load.wait()
    numbers = [
        jnp.where(
            jnp.full((1, TILE), count_ref[0, 0], jnp.int32) > s,
            jnp.full((1, TILE), list_ref[0, 0, s], jnp.int32),
            -1,
        )
        for s in range(live)
    ]
    for t in range(tiles):
        place = jnp.full((1, TILE), live, jnp.int32)
        for s in range(live):
            place = jnp.where(numbers[s] == t, s, place)
        slots[col, pl.ds(t, 1), :] = place
    place_copy(col).start()
    for load in amp_loads:
        load.wait()
    for s in range(live):
        packed[col, s] = amp[list_ref[0, 0, s]]

    peers = 2
    for _, exists in partners[2:]:
        peers += jnp.where(exists, 1, 0)
    pl.semaphore_wait(barrier, peers)

    def send_own_amp(copy):
        pl.when(has_above)(lambda: copy(0, above).start())
        pl.when(has_below)(lambda: copy(1, below).start())
        copy(2, sibling).start()

    def send_row(source, at, count=1):
        pl.when(has_right)(lambda: int_copy(source, at, 0, right, count).start())
        pl.when(has_left)(lambda: int_copy(source, at, 1, left, count).start())

    send_own_amp(lambda way, target: slot_copy(col, way, target))
    for s in range(len(groups)):
        send_own_amp(lambda way, target, s=s: amp_copy(col, s, way, target))

    for at in range(2 * pieces):
        int_loads[at].wait()
        span = pl.ds(at * piece, piece)
        for c in range(int_cols // TILE):
            keep = mask_ref[c, at * piece // TILE].astype(F32)
            cols = pl.ds(c * TILE, TILE)
            ints[pair, span, cols] = ints[pair, span, cols] * keep

    for u in range(pieces):
        send_row(pair, u)
        int_copy(pair, pieces + u, 2, across).start()
    send_row(pair, pieces, pieces)
    int_copy(pair, 0, 2, across, pieces).start()

    out_ref[...] = jnp.zeros_like(out_ref)

    def amp_slot(source):
        return jnp.abs(div(source, CORES) - line_at)

    def int_slot(source, part):
        away = jnp.abs(rem(source, wide) - low_at)
        same = div(source, wide) == high_at
        near = jnp.where(part == 0, away, jnp.where(away > 0, away + 1, 0))
        far = jnp.where(part == 0, away + 2, jnp.where(away > 0, away + 2, 1))
        return jnp.where(same, near, far)

    steps = max(line - 1, wide + 1)

    def drain_amp(source, way, target):
        slot_copy(source, way, target).wait_send()
        for s in range(len(groups)):
            amp_copy(source, s, way, target).wait_send()

    def drain_early():
        @pl.loop(0, n_col)
        def _(source):
            mine = rem(source, CORES) == core
            at = div(source, CORES)

            when(mine, at <= line_at, has_above)(lambda: drain_amp(source, 0, above))
            when(mine, at >= line_at, has_below)(lambda: drain_amp(source, 1, below))
            when(mine, jnp.abs(at - line_at) < steps)(lambda: drain_amp(source, 2, sibling))

        @pl.loop(0, n_pair)
        def _(source):
            same = div(source, wide) == high_at
            at = rem(source, wide)

            def drain(first, way, target, count=1):
                for u in range(0, pieces, count):
                    int_copy(source, first + u, way, target, count).wait_send()

            to_right, to_left = (at <= low_at, has_right), (at >= low_at, has_left)
            when(same, *to_right)(lambda: drain(0, 0, right))
            when(same, *to_left)(lambda: drain(0, 1, left))
            when(same, at != low_at)(lambda: drain(0, 2, across))
            when(same, at == low_at)(lambda: drain(0, 2, across, pieces))
            when(same, *to_right)(lambda: drain(pieces, 0, right, pieces))
            when(same, *to_left)(lambda: drain(pieces, 1, left, pieces))
            when(~same, *to_right)(lambda: drain(pieces, 0, right))
            when(~same, *to_left)(lambda: drain(pieces, 1, left))
            pl.when(source == pair)(lambda: drain(pieces, 2, across))

    def step(now, _):
        pl.when(now == steps)(drain_early)

        def pass_amp(source, exists, way, target, more):
            @when(now >= 1, exists)
            def _():
                slot_copy(source, way, target).wait_recv()
                place_copy(source).start()
                pl.when(more)(lambda: slot_copy(source, way, target).start())
                slot_copy(source, 2, sibling).start()

        def pass_tile(source, s, exists, way, target, more):
            @when(now >= 1, exists)
            def _():
                amp_copy(source, s, way, target).wait_recv()
                pl.when(more)(lambda: amp_copy(source, s, way, target).start())
                amp_copy(source, s, 2, sibling).start()

        def pass_row(source, at, away, across_too, count=1):
            def one(side, exists, way, target, more):
                origin = source + side * away

                @when(away >= 1, exists)
                def _():
                    int_copy(origin, at, way, target, count).wait_recv()
                    pl.when(more)(lambda: int_copy(origin, at, way, target, count).start())
                    if across_too:
                        int_copy(origin, at, 2, across).start()

            one(-1, low_at - away >= 0, 0, right, has_right)
            one(1, low_at + away < wide, 1, left, has_left)

        lower, upper = col - CORES * now, col + CORES * now
        pass_amp(lower, line_at - now >= 0, 0, above, has_above)
        pass_amp(upper, line_at + now < line, 1, below, has_below)
        other = (1 - high_at) * wide + low_at
        for s in range(max(len(groups), pieces)):
            if s < len(groups):
                pass_tile(lower, s, line_at - now >= 0, 0, above, has_above)
                pass_tile(upper, s, line_at + now < line, 1, below, has_below)
            if s < pieces:
                pass_row(pair, s, now, True)

                @when(now == 1)
                def _(s=s):
                    int_copy(other, pieces + s, 2, across).wait_recv()
                    send_row(other, pieces + s)

        away = now - 2
        pass_row(pair, pieces, now - 1, False, pieces)
        pl.when(away == 0)(lambda: int_copy(other, 0, 2, across, pieces).wait_recv())
        for u in range(pieces):
            pass_row(other, pieces + u, away, False)
            for side, exists in ((-1, low_at - away >= 0), (1, low_at + away < wide)):
                @when(away >= 1, exists)
                def _(side=side, u=u):
                    int_copy(other + side * away, u, 2, across).wait_recv()

        def from_sibling(source):
            slot_copy(source, 2, sibling).wait_recv()
            place_copy(source).start()
            for s in range(len(groups)):
                amp_copy(source, s, 2, sibling).wait_recv()

        @pl.loop(0, n_pair * 2)
        def _(block):
            source, part = div(block, 2), rem(block, 2)

            @pl.when(int_slot(source, part) == now)
            def _():
                span = pl.ds(pl.multiple_of(part * half, half), half)
                value = ints[source, span]
                b_high[source, span], b_low[source, span] = split(value)

        mate = line_at * CORES + 1 - core

        @pl.loop(0, CORES)
        def _(turn):
            @pl.when(turn == 1)
            def _():
                pl.when(line_at - now >= 0)(lambda: from_sibling(mate - CORES * now))
                when(now >= 1, line_at + now < line)(lambda: from_sibling(mate + CORES * now))

            other_core = rem(core + turn, CORES)

            @pl.loop(0, 2)
            def _(side):
                place_at = line_at + (2 * side - 1) * now
                source = place_at * CORES + other_core

                @when(place_at >= 0, place_at < line, (side == 0) | (now > 0))
                def _():
                    for s in range(live):
                        part_high[s], part_low[s] = split(packed[source, s])
                    place_copy(source).wait()
                    for t in range(tiles):
                        place = place_ref[source, t, 0]
                        a_high[(source, *tile_at(t))] = part_high[place]
                        a_low[(source, *tile_at(t))] = part_low[place]

            @pl.loop(0, line)
            def _(place_at):
                source = place_at * CORES + other_core
                start = source * depth
                origin, offset = div(start, int_rows), rem(start, int_rows)
                due = jnp.maximum(amp_slot(source), int_slot(origin, div(offset, half)))

                @pl.when(due == now)
                def _():
                    span = pl.ds(pl.multiple_of(offset, depth), depth)
                    high, low = b_high[origin, span], b_low[origin, span]
                    first = a_high[source]
                    total = jnp.dot(first, high, preferred_element_type=F32)
                    total += jnp.dot(first, low, preferred_element_type=F32)
                    total += jnp.dot(a_low[source], high, preferred_element_type=F32)
                    out_ref[...] += total

        return 0

    lax.fori_loop(0, steps + 1, step, 0)

    for side in (-1, 1):
        ending = line_at + side * steps

        @when(ending >= 0, ending < line)
        def _(ending=ending):
            drain_amp(ending * CORES + core, 2, sibling)


def local(n_pair, n_col, amplitudes, integrals, amp_tiles, amp_count, int_mask):
    rows, depth = amplitudes.shape
    int_rows, int_cols = integrals.shape
    live = amp_tiles.shape[-1]
    tiles = (rows // TILE) * (depth // TILE)
    half = int_rows // 2
    assert n_pair % 2 == 0 and n_col % CORES == 0
    assert half % depth == 0 and half % TILE == 0
    pieces = int_rows // TILE
    scratch = [
        pltpu.SMEM(amp_tiles.shape, jnp.int32),
        pltpu.SMEM(amp_count.shape, jnp.int32),
        pltpu.SMEM(int_mask.shape[::-1], jnp.int32),
        pltpu.SMEM((n_col, tiles, TILE), jnp.int32),
        pltpu.VMEM((tiles, TILE, TILE), F32),
        pltpu.VMEM((live + 1, TILE, TILE), BF16),
        pltpu.VMEM((live + 1, TILE, TILE), BF16),
        pltpu.VMEM((n_col, live, TILE, TILE), F32),
        pltpu.VMEM((n_col, tiles, TILE), jnp.int32),
        pltpu.VMEM((n_pair, int_rows, int_cols), F32),
        pltpu.VMEM((n_col, rows, depth), BF16),
        pltpu.VMEM((n_col, rows, depth), BF16),
        pltpu.VMEM((n_pair, int_rows, int_cols), BF16),
        pltpu.VMEM((n_pair, int_rows, int_cols), BF16),
        pltpu.SemaphoreType.DMA((3,)),
        pltpu.SemaphoreType.DMA((tiles,)),
        pltpu.SemaphoreType.DMA((pieces,)),
        pltpu.SemaphoreType.DMA((n_col,)),
        pltpu.SemaphoreType.DMA((n_col, live)),
        pltpu.SemaphoreType.DMA((3, n_col, live)),
        pltpu.SemaphoreType.DMA((n_col,)),
        pltpu.SemaphoreType.DMA((3, n_col)),
        pltpu.SemaphoreType.DMA((n_pair, pieces)),
        pltpu.SemaphoreType.DMA((3, n_pair, pieces)),
    ]
    return pl.pallas_call(
        functools.partial(kernel, n_pair, n_col),
        out_shape=pltpu.VMEM((rows, int_cols), F32),
        in_specs=[pl.BlockSpec(memory_space=pltpu.HBM)] * 5,
        out_specs=pl.BlockSpec(memory_space=pltpu.VMEM),
        scratch_shapes=scratch,
        compiler_params=pltpu.CompilerParams(
            collective_id=0, has_side_effects=True, vmem_limit_bytes=VMEM_BYTES
        ),
        cost_estimate=pl.CostEstimate(
            flops=6 * rows * depth * n_col * int_cols,
            bytes_accessed=4 * rows * (2 * depth + int_cols),
            transcendentals=0,
        ),
        name="ladder",
    )(amp_tiles, amp_count, int_mask.T, amplitudes, integrals)


def solution(mesh):
    return jax.shard_map(
        functools.partial(local, mesh.shape["pair"], mesh.shape["col"]),
        mesh=mesh,
        in_specs=(
            P("pair", "col"),
            P("pair", "col"),
            P("pair", "col", None),
            P("pair", "col"),
            P("pair", "col"),
        ),
        out_specs=P("pair", "col"),
        check_vma=False,
    )
```
